128 devices in a mesh: tm: 16 (over y, z), rows: 8 (over x, core).
Axes of the slice: x: 4, y: 4, z: 4, core: 2. Of those that a mesh axis runs over, the one named last changes fastest.
Arguments:
- feat: bfloat16 [64, 128, 128, 256], P('tm', 'rows')
- gamma: float32 [256], replicated, may hold values from 0.1 to 1.9
- beta: float32 [256], replicated, may hold values from -3 to 3
- conv_weight: bfloat16 [3, 3, 768, 256], replicated, may hold values from -0.078125 to 0.078125
- conv_bias: float32 [256], replicated, may hold values from -3 to 3
- proj: bfloat16 [256, 16], replicated, may hold values from -0.375 to 0.375
- proj_bias: float32 [16], replicated, may hold values from -3 to 3
- clip_len: int32 [16], replicated, may hold values from 1 to 8, 64 in all
- owner: int32 [16], replicated, may hold values from 0 to 15, as said below
Outputs:
- block: bfloat16 [64, 128, 128, 256], P('tm', 'rows')
- latent_seq: bfloat16 [128, 128, 2048], P('tm', 'rows')
The draws below stay inside these ranges and needn't reach their ends.
Inputs may be any that keep to these rules, and one draw needn't show every extreme that they name: `clip_len`: the lengths sum to 64; the longest clip has exactly 8 frames. `owner`: each tm index owns exactly one clip.
All inputs are finite; a program needn't handle non-finite values.
Results may differ from the reference program's by a relative error of at most 0.0052.
Values may be sent and summed in bfloat16 or wider, within the bound.
No kernel may reach another device: no remote copies, remote signals or barrier semaphores. Data moves between devices by JAX's collectives and lax.ppermute only.
A program may use at most 256 MiB of HBM per device.

```python
import math
import jax
import jax.numpy as jnp
import numpy as np
from jax import lax

C = 256
GROUPS = 32
Z = 16
W = 128
NF = 64
NH = 128
CLIPS = 16
SEQ_CAP = 8


def draw_feat(key, part):
    key = jax.random.fold_in(key, 11)
    key_noise, key_scale, key_shift = jax.random.split(key, 3)
    scale = jnp.exp(jax.random.uniform(key_scale, (NF, 1, 1, 1), jnp.float32, math.log(0.5), math.log(2.0)))
    shift = jax.random.uniform(key_shift, (NF, 1, 1, C), jnp.float32, -1.0, 1.0)
    noise = jax.random.normal(key_noise, (NF, NH, W, C), jnp.float32)
    return (noise * scale + shift).astype(jnp.bfloat16)


def draw_owner(key, part):
    key = jax.random.fold_in(key, 23)
    return jax.random.permutation(key, CLIPS).astype(jnp.int32)


def length_profile(count, total, limit, slope):
    loads = [(1 << 20) // math.isqrt(grade ** slope) + 1 for grade in range(2, count + 1)]
    rest, counts = total - limit - (count - 1), [1] * (count - 1)
    while rest > 0:
        movable = [i for i in range(count - 1) if counts[i] < limit]
        mass, remaining = sum([loads[i] for i in movable]), rest
        for i in movable:
            more = min(limit - counts[i], max(1, remaining * loads[i] // mass), rest)
            counts[i] = counts[i] + more
            rest = rest - more
    return np.array([limit] + counts)


def ragged(key, count, total, reach, slope):
    if count == 2:
        one = jax.random.randint(key, (), max(1, total - reach), min(reach, total - 1) + 1)
        return jnp.stack([one, total - one])
    tallies = jnp.asarray(length_profile(count, total, reach, slope), jnp.int32)
    couples = (count - 1) // 2
    source_of, receiver = tallies[1:1 + 2 * couples:2], tallies[2:2 + 2 * couples:2]
    room = jnp.minimum(source_of - 1, reach - receiver)
    passed = jax.random.randint(jax.random.fold_in(key, 1), (couples,), 0, 1 << 20) % (room + 1)
    tallies = tallies.at[1:1 + 2 * couples:2].set(source_of - passed).at[2:2 + 2 * couples:2].set(receiver + passed)
    return tallies[jax.random.permutation(jax.random.fold_in(key, 2), count)]


def scatter_about(stream_key, extent, scale, bound, held_as=jnp.bfloat16):
    return jnp.clip(scale * jax.random.normal(stream_key, extent, jnp.float32), -bound, bound).astype(held_as)


def setup_inputs(seed: int = 0) -> dict:
    seeds = jax.random.split(jax.random.key(seed), 10)
    return {
        "feat": draw_feat(jax.random.fold_in(seeds[9], 71), 0),
        "gamma": jnp.clip(1.0 + 0.18 * jax.random.normal(seeds[1], (C,), jnp.float32), 0.1, 1.9),
        "beta": scatter_about(seeds[2], (C,), 0.5, 3.0, jnp.float32),
        "conv_weight": scatter_about(seeds[3], (3, 3, 3 * C, C), (27 * C) ** -0.5, 0.078125),
        "conv_bias": scatter_about(seeds[4], (C,), 0.5, 3.0, jnp.float32),
        "proj": scatter_about(seeds[5], (C, Z), C ** -0.5, 0.375),
        "proj_bias": scatter_about(seeds[6], (Z,), 0.5, 3.0, jnp.float32),
        "clip_len": ragged(seeds[7], CLIPS, NF, SEQ_CAP, 2).astype(jnp.int32),
        "owner": draw_owner(jax.random.fold_in(seeds[9], 71), 0),
    }


def clip_tables(clip_len, frame_ids):
    ends = jnp.cumsum(clip_len).astype(jnp.int32)
    starts = (ends - clip_len).astype(jnp.int32)
    clip_of = lax.optimization_barrier(jnp.sum((frame_ids[:, None] >= ends[None, :]).astype(jnp.int32), axis=1)).astype(jnp.int32)
    member_int = (clip_of[None, :] == jnp.arange(CLIPS, dtype=jnp.int32)[:, None]).astype(jnp.int32)
    frame_start = lax.optimization_barrier(jnp.sum(member_int * starts[:, None], axis=0)).astype(jnp.int32)
    return (member_int.astype(jnp.float32), member_int, frame_start)

def moments(feat):
    frames, height, width, chans = feat.shape
    grouped = feat.astype(jnp.float32).reshape(frames, height, width, GROUPS, chans // GROUPS)
    return (lax.optimization_barrier(jnp.sum(grouped, axis=(1, 2, 4))), lax.optimization_barrier(jnp.sum(grouped * grouped, axis=(1, 2, 4))))

def normalize(feat, gamma, beta, member, tot_one, tot_two, count):
    chans = feat.shape[3]
    mean = tot_one / count
    var = tot_two / count - mean * mean
    inv = lax.rsqrt(var + 1e-06)
    frame_mean = jnp.dot(member.T, mean, precision=lax.Precision.HIGHEST)
    frame_inv = jnp.dot(member.T, inv, precision=lax.Precision.HIGHEST)
    frame_mean = jnp.repeat(frame_mean, chans // GROUPS, axis=1)[:, None, None, :]
    frame_inv = jnp.repeat(frame_inv, chans // GROUPS, axis=1)[:, None, None, :]
    normed = (feat.astype(jnp.float32) - frame_mean) * frame_inv * gamma + beta
    return jax.nn.silu(normed).astype(jnp.bfloat16)

def conv_frame(frames, conv_weight):
    height, width, chans = (frames.shape[1], frames.shape[2], frames.shape[3])
    padded = jnp.pad(frames, ((0, 0), (1, 1), (1, 1), (0, 0)))
    total = jnp.zeros((height * width, chans), jnp.float32)
    for tap_time in range(3):
        for tap_row in range(3):
            columns = jnp.concatenate([padded[tap_time, tap_row:tap_row + height, tap_col:tap_col + width] for tap_col in range(3)], axis=-1)
            total = total + jnp.dot(columns.reshape(-1, 3 * chans), conv_weight[tap_time, tap_row], preferred_element_type=jnp.float32)
    return total.reshape(height, width, chans)

def reference(feat, gamma, beta, conv_weight, conv_bias, proj, proj_bias, clip_len, owner):
    frames, height, width, chans = feat.shape
    latent_ch = proj.shape[1]
    frame_ids = jnp.arange(frames, dtype=jnp.int32)
    member, member_int, frame_start = clip_tables(clip_len, frame_ids)
    one, two = moments(feat)
    tot_one = jnp.dot(member, one, precision=lax.Precision.HIGHEST)
    tot_two = jnp.dot(member, two, precision=lax.Precision.HIGHEST)
    count = (clip_len.astype(jnp.float32) * float(height * width * (chans // GROUPS)))[:, None]
    hidden = normalize(feat, gamma, beta, member, tot_one, tot_two, count)
    sources = jnp.maximum(frame_ids[:, None] - 2 + jnp.arange(3, dtype=jnp.int32)[None, :], frame_start[:, None]).astype(jnp.int32)

    def one_frame(index):
        picked = jnp.take(hidden, sources[index], axis=0)
        summed = conv_frame(picked, conv_weight)
        return (feat[index].astype(jnp.float32) + summed + conv_bias).astype(jnp.bfloat16)
    block = lax.map(one_frame, frame_ids)
    latent = (jnp.dot(block.reshape(-1, chans), proj, preferred_element_type=jnp.float32) + proj_bias).astype(jnp.bfloat16)
    latent = latent.reshape(frames, height, width * latent_ch)
    frame_owner = lax.optimization_barrier(jnp.sum(member_int * owner[:, None], axis=0)).astype(jnp.int32)
    target = (frame_owner * SEQ_CAP + frame_ids - frame_start).astype(jnp.int32)
    latent_seq = jnp.zeros((CLIPS * SEQ_CAP, height, width * latent_ch), jnp.bfloat16).at[target].set(latent)
    return (block, latent_seq)
```

```python
import jax
import jax.numpy as jnp
from jax import lax
from jax.experimental import pallas as pl
from jax.experimental.pallas import tpu as pltpu
from jax.sharding import PartitionSpec as P

GROUPS = 32
SEQ_CAP = 8
F32 = jnp.float32
BF16 = jnp.bfloat16
MIB = 2**20


def stats_kernel(x_ref, o_ref):
    f = pl.program_id(0)
    x = x_ref[0].astype(F32)
    x = x.reshape(-1, 8, x.shape[-1])
    one = jnp.sum(jnp.sum(x, axis=0), axis=0, keepdims=True)
    two = jnp.sum(jnp.sum(x * x, axis=0), axis=0, keepdims=True)
    o_ref[pl.ds(f, 1), :] = one
    o_ref[pl.ds(4 + f, 1), :] = two


def channel_stats(feat):
    frames, band, width, chans = feat.shape
    return pl.pallas_call(
        stats_kernel,
        grid=(frames,),
        in_specs=[pl.BlockSpec((1, band, width, chans), lambda f: (f, 0, 0, 0))],
        out_specs=pl.BlockSpec((2 * frames, chans), lambda f: (0, 0)),
        out_shape=jax.ShapeDtypeStruct((2 * frames, chans), F32),
        compiler_params=pltpu.CompilerParams(vmem_limit_bytes=24 * MIB),
        cost_estimate=pl.CostEstimate(
            flops=4 * feat.size, bytes_accessed=2 * feat.size, transcendentals=0
        ),
        name="channel_stats",
    )(feat)


def normed_rows(x, half_scale, half_shift):
    u = x.astype(F32) * half_scale + half_shift
    return u + u * jnp.tanh(u)


def put_rows(slab, row, h):
    width, chans = h.shape
    col = lax.broadcasted_iota(jnp.int32, h.shape, 0)
    left = jnp.where(col == 0, 0.0, pltpu.roll(h, 1, 0))
    right = jnp.where(col == width - 1, 0.0, pltpu.roll(h, width - 1, 0))
    slab[row, :, 0:chans] = left.astype(BF16)
    slab[row, :, chans : 2 * chans] = h.astype(BF16)
    slab[row, :, 2 * chans :] = right.astype(BF16)


def tap_dots(total, slab, weights, row, rows):
    for tap_row in range(3):
        lhs = slab[pl.ds(row + tap_row, rows)]
        lhs = lhs.reshape(rows * lhs.shape[1], lhs.shape[2])
        total = total + jnp.dot(lhs, weights[tap_row], preferred_element_type=F32)
    return total


def latent_frame(block, projt_ref, pbias_ref, lscr, lat_ref, f):
    rows, width, chans = block.shape
    wide = projt_ref.shape[1]
    per = wide // 16
    both = jnp.dot(
        block.reshape(rows * width, chans), projt_ref[...], preferred_element_type=F32
    ).reshape(rows, width, wide)
    col = lax.broadcasted_iota(jnp.int32, both.shape, 1)
    lane = lax.broadcasted_iota(jnp.int32, both.shape, 2)
    lscr[...] = jnp.where(col % per == lane // 16, both, 0.0)
    for j in range(width // per):
        part = jnp.sum(lscr[:, per * j : per * (j + 1), :], axis=1) + pbias_ref[...]
        lat_ref[j, f] = part.astype(BF16)


def local_kernel(
    starts, edges, feat_hbm, top_hbm, bot_hbm, w_hbm, sums_ref, mask_ref, count_ref,
    group_ref, gamma_ref, beta_ref, cbias_ref, projt_ref, pbias_ref,
    block_hbm, part_hbm, lat_ref, affine_ref,
    feat, halo, w, slab, obuf, part, lscr, sems, osems,
):
    copies = [pltpu.make_async_copy(feat_hbm.at[f], feat.at[f], sems.at[f]) for f in range(4)]
    top_copy = pltpu.make_async_copy(top_hbm, halo.at[0], sems.at[4])
    bot_copy = pltpu.make_async_copy(bot_hbm, halo.at[1], sems.at[5])
    w_copy = pltpu.make_async_copy(w_hbm, w, sems.at[6])
    top_copy.start()
    bot_copy.start()
    for c in copies:
        c.start()
    w_copy.start()

    tot = jnp.dot(
        mask_ref[...], sums_ref[...], precision=lax.Precision.HIGHEST, preferred_element_type=F32
    )
    tot = jnp.dot(
        tot, group_ref[...], precision=lax.Precision.HIGHEST, preferred_element_type=F32
    )
    mom = tot / count_ref[...]
    mean = mom[0:4]
    var = mom[4:8] - mean * mean
    scale = lax.rsqrt(var + 1e-06) * gamma_ref[...]
    affine_ref[0:4] = 0.5 * scale
    affine_ref[4:8] = 0.5 * (beta_ref[...] - mean * scale)

    top_copy.wait()
    bot_copy.wait()
    for f in range(4):
        copies[f].wait()
        hs = affine_ref[f : f + 1]
        hb = affine_ref[4 + f : 5 + f]
        page = slab.at[f]
        top_on = (edges[0] > 0).astype(F32)
        bot_on = (edges[1] > 0).astype(F32)
        put_rows(page, 0, normed_rows(halo[0, f], hs, hb) * top_on)
        put_rows(page, 17, normed_rows(halo[1, f], hs, hb) * bot_on)

        def norm_row(r, _, f=f, hs=hs, hb=hb, page=page):
            put_rows(page, r + 1, normed_rows(feat[f, r], hs, hb))
            return 0

        lax.fori_loop(0, 16, norm_row, 0, unroll=2)
    w_copy.wait()

    rows = 8
    zero = jnp.zeros((rows * 128, 256), F32)
    outs = []
    for f in (3, 2):
        src = [jnp.maximum(f - 2 + a, starts[f]) for a in range(3)]

        def chunk(m, _, f=f, src=src):
            total = zero
            for a in range(3):
                total = tap_dots(total, slab.at[src[a]], w.at[a], m * rows, rows)
            total = total.reshape(rows, 128, 256)
            r = pl.ds(m * rows, rows)
            obuf[f - 2, r] = (total + feat[f, r].astype(F32) + cbias_ref[...]).astype(BF16)
            return 0

        lax.fori_loop(0, 2, chunk, 0)
        c = pltpu.make_async_copy(obuf.at[f - 2], block_hbm.at[f], osems.at[f - 2])
        c.start()
        outs.append(c)
        latent_frame(obuf[f - 2], projt_ref, pbias_ref, lscr, lat_ref, f - 2)

    src1 = jnp.maximum(0, starts[1])

    def chunk1(m, _):
        total = tap_dots(zero, slab.at[1], w.at[2], m * rows, rows)
        total = tap_dots(total, slab.at[src1], w.at[1], m * rows, rows)
        part[1, pl.ds(m * rows, rows)] = total.reshape(rows, 128, 256)
        return 0

    lax.fori_loop(0, 2, chunk1, 0)

    def chunk0(m, _):
        total = tap_dots(zero, slab.at[0], w.at[2], m * rows, rows)
        part[0, pl.ds(m * rows, rows)] = total.reshape(rows, 128, 256)
        return 0

    lax.fori_loop(0, 2, chunk0, 0)

    @pl.when(starts[1] >= 0)
    def _():
        def more(m, _):
            r = pl.ds(m * rows, rows)
            total = part[1, r].reshape(rows * 128, 256)
            total = tap_dots(total, slab.at[src1], w.at[0], m * rows, rows)
            part[1, r] = total.reshape(rows, 128, 256)
            return 0

        lax.fori_loop(0, 2, more, 0)

    @pl.when(starts[0] >= 0)
    def _():
        def more(m, _):
            r = pl.ds(m * rows, rows)
            total = part[0, r].reshape(rows * 128, 256)
            total = tap_dots(total, slab.at[0], w.at[0], m * rows, rows)
            total = tap_dots(total, slab.at[0], w.at[1], m * rows, rows)
            part[0, r] = total.reshape(rows, 128, 256)
            return 0

        lax.fori_loop(0, 2, more, 0)

    for f in range(2):
        c = pltpu.make_async_copy(part.at[f], part_hbm.at[f], osems.at[2 + f])
        c.start()
        outs.append(c)
    for c in outs:
        c.wait()


ANY = pl.BlockSpec(memory_space=pl.ANY)
VM = pl.BlockSpec(memory_space=pltpu.VMEM)
SM = pl.BlockSpec(memory_space=pltpu.SMEM)


def local_part(starts, edges, feat, top, bot, weight, sums, mask, count, group, gamma, beta,
               cbias, projt, pbias):
    shape = feat.shape
    return pl.pallas_call(
        local_kernel,
        in_specs=[SM, SM, ANY, ANY, ANY, ANY] + [VM] * 9,
        out_specs=[ANY, ANY, VM, VM],
        out_shape=[
            jax.ShapeDtypeStruct(shape, BF16),
            jax.ShapeDtypeStruct((2,) + shape[1:], F32),
            jax.ShapeDtypeStruct((16, 2, 16, 128), BF16),
            jax.ShapeDtypeStruct((8, 256), F32),
        ],
        scratch_shapes=[
            pltpu.VMEM(shape, BF16),
            pltpu.VMEM((2, 4, 128, 256), BF16),
            pltpu.VMEM(weight.shape, BF16),
            pltpu.VMEM((4, 18, 128, 768), BF16),
            pltpu.VMEM((2, 16, 128, 256), BF16),
            pltpu.VMEM((2, 16, 128, 256), F32),
            pltpu.VMEM((16, 128, 128), F32),
            pltpu.SemaphoreType.DMA((7,)),
            pltpu.SemaphoreType.DMA((4,)),
        ],
        compiler_params=pltpu.CompilerParams(vmem_limit_bytes=56 * MIB),
        cost_estimate=pl.CostEstimate(
            flops=2 * 9 * 2048 * 2304 * 256, bytes_accessed=16 * MIB, transcendentals=feat.size
        ),
        name="local_conv",
    )(starts, edges, feat, top, bot, weight, sums, mask, count, group, gamma, beta, cbias, projt,
      pbias)


def past_kernel(
    starts, edges, one_ref, two_ref, border_ref, top_ref, bot_ref, feat_hbm, w_hbm, part_hbm,
    affine_ref, cbias_ref, projt_ref, pbias_ref, early_ref, block_in,
    block_hbm, lat_ref,
    feat, w, slab, obuf, part, lscr, sems, osems,
):
    del block_in
    copies = [
        pltpu.make_async_copy(w_hbm.at[pl.ds(0, 2)], w, sems.at[0]),
        pltpu.make_async_copy(part_hbm, part, sems.at[1]),
        pltpu.make_async_copy(feat_hbm.at[pl.ds(0, 2)], feat, sems.at[2]),
    ]
    for c in copies:
        c.start()
    hs = affine_ref[0:1]
    hb = affine_ref[4:5]
    top_on = (edges[0] > 0).astype(F32)
    bot_on = (edges[1] > 0).astype(F32)
    mains = (two_ref, one_ref)
    for p in range(2):
        @pl.when(starts[0] < p - 1)
        def _(p=p):
            page = slab.at[p]
            put_rows(page, 0, normed_rows(top_ref[p], hs, hb) * top_on)
            put_rows(page, 1, normed_rows(border_ref[p, 0], hs, hb))
            put_rows(page, 16, normed_rows(border_ref[p, 1], hs, hb))
            put_rows(page, 17, normed_rows(bot_ref[p], hs, hb) * bot_on)

            def norm_row(r, _):
                put_rows(page, r + 2, normed_rows(mains[p][r], hs, hb))
                return 0

            lax.fori_loop(0, 14, norm_row, 0, unroll=2)
    for c in copies:
        c.wait()
    rows = 8

    @pl.when(starts[1] < 0)
    def _():
        def more(m, _):
            r = pl.ds(m * rows, rows)
            total = part[1, r].reshape(rows * 128, 256)
            total = tap_dots(total, slab.at[1], w.at[0], m * rows, rows)
            part[1, r] = total.reshape(rows, 128, 256)
            return 0

        lax.fori_loop(0, 2, more, 0)

    src0 = jnp.clip(starts[0] + 2, 0, 1)

    @pl.when(starts[0] < 0)
    def _():
        def more(m, _):
            r = pl.ds(m * rows, rows)
            total = part[0, r].reshape(rows * 128, 256)
            total = tap_dots(total, slab.at[1], w.at[1], m * rows, rows)
            total = tap_dots(total, slab.at[src0], w.at[0], m * rows, rows)
            part[0, r] = total.reshape(rows, 128, 256)
            return 0

        lax.fori_loop(0, 2, more, 0)

    outs = []
    for f in (1, 0):
        def finish(r, _, f=f):
            rr = pl.ds(r * 2, 2)
            obuf[f, rr] = (part[f, rr] + feat[f, rr].astype(F32) + cbias_ref[...]).astype(BF16)
            return 0

        lax.fori_loop(0, 8, finish, 0)
        c = pltpu.make_async_copy(obuf.at[f], block_hbm.at[f], osems.at[f])
        c.start()
        outs.append(c)
        latent_frame(obuf[f], projt_ref, pbias_ref, lscr, lat_ref, f)
    lat_ref[:, 2:4] = early_ref[...]
    for c in outs:
        c.wait()


def past_part(starts, edges, one, two, border, top, bot, feat, weight, part, affine, cbias, projt,
              pbias, early, block):
    shape = feat.shape
    return pl.pallas_call(
        past_kernel,
        in_specs=[SM, SM] + [VM] * 5 + [ANY] * 3 + [VM] * 5 + [ANY],
        out_specs=[ANY, VM],
        out_shape=[
            jax.ShapeDtypeStruct(shape, BF16),
            jax.ShapeDtypeStruct((16, 4, 16, 128), BF16),
        ],
        input_output_aliases={15: 0},
        scratch_shapes=[
            pltpu.VMEM((2,) + shape[1:], BF16),
            pltpu.VMEM((2,) + weight.shape[1:], BF16),
            pltpu.VMEM((2, 18, 128, 768), BF16),
            pltpu.VMEM((2, 16, 128, 256), BF16),
            pltpu.VMEM((2, 16, 128, 256), F32),
            pltpu.VMEM((16, 128, 128), F32),
            pltpu.SemaphoreType.DMA((3,)),
            pltpu.SemaphoreType.DMA((2,)),
        ],
        compiler_params=pltpu.CompilerParams(vmem_limit_bytes=56 * MIB),
        cost_estimate=pl.CostEstimate(
            flops=2 * 3 * 2048 * 2304 * 256, bytes_accessed=12 * MIB, transcendentals=feat.size // 2
        ),
        name="past_conv",
    )(starts, edges, one, two, border, top, bot, feat, weight, part, affine, cbias, projt, pbias,
      early, block)


def place_kernel(codes, x_ref, o_ref):
    o_ref[...] = jnp.zeros_like(o_ref)

    def put(t, _):
        o_ref[codes[t]] = x_ref[t]
        return 0

    lax.fori_loop(0, x_ref.shape[0], put, 0, unroll=8)


def place(codes, shares):
    return pl.pallas_call(
        place_kernel,
        in_specs=[SM, VM],
        out_specs=VM,
        out_shape=jax.ShapeDtypeStruct((128, 16, 128), BF16),
        name="place_frames",
    )(codes, shares)


def merge_kernel(x_ref, o_ref):
    for j in range(x_ref.shape[0]):
        o_ref[:, :, 128 * j : 128 * (j + 1)] = x_ref[j]


def merge(seq):
    return pl.pallas_call(
        merge_kernel,
        in_specs=[VM],
        out_specs=VM,
        out_shape=jax.ShapeDtypeStruct((8, 16, 2048), BF16),
        name="merge_columns",
    )(seq)


def clip_tables(clip_len, frame_ids):
    ends = jnp.cumsum(clip_len)
    starts = ends - clip_len
    clip_of = jnp.sum((frame_ids[:, None] >= ends[None, :]).astype(jnp.int32), axis=1)
    member = (clip_of[:, None] == jnp.arange(clip_len.shape[0], dtype=jnp.int32)[None, :]).astype(
        jnp.int32
    )
    return clip_of, member, jnp.sum(member * starts[None, :], axis=1)


def swap(x, axis, bit):
    n = lax.axis_size(axis)
    return lax.ppermute(x, axis, [(i, i ^ bit) for i in range(n)])


def shift(x, axis, by):
    n = lax.axis_size(axis)
    return lax.ppermute(x, axis, [(i, i + by) for i in range(n) if 0 <= i + by < n])


def on_device(feat, gamma, beta, conv_weight, conv_bias, proj, proj_bias, clip_len, owner):
    frames, band, width, chans = feat.shape
    latent_ch = proj.shape[1]
    n_time = lax.axis_size("tm")
    n_bands = lax.axis_size("rows")
    tm = lax.axis_index("tm")
    row = lax.axis_index("rows")

    border = shift(jnp.stack([feat[2:, 0], feat[2:, band - 1]], axis=1), "tm", 1)
    past_one = shift(feat[3, 1 : band - 1], "tm", 1)
    past_two = shift(feat[2, 1 : band - 1], "tm", 1)
    top = shift(feat[:, band - 1], "rows", 1)
    bot = shift(feat[:, 0], "rows", -1)
    past_top = shift(border[:, 1], "rows", 1)
    past_bot = shift(border[:, 0], "rows", -1)

    ids = tm * frames + jnp.arange(frames, dtype=jnp.int32)
    clip_of, member, start = clip_tables(clip_len, ids)
    local_start = (start - tm * frames).astype(jnp.int32)
    edges = jnp.stack([row, n_bands - 1 - row]).astype(jnp.int32)
    window = jnp.stack([tm, tm ^ 1, tm - 2, (tm - 2) ^ 1, tm + 2, (tm + 2) ^ 1])
    window_ids = (window[:, None] * frames + jnp.arange(frames)[None, :]).reshape(-1)
    window_clip, _, _ = clip_tables(clip_len, window_ids.astype(jnp.int32))
    same = (clip_of[:, None] == window_clip[None, :]).astype(F32).reshape(frames, 6, frames)
    none = jnp.zeros_like(same)
    mask = jnp.concatenate(
        [jnp.stack([same, none], axis=2), jnp.stack([none, same], axis=2)], axis=0
    ).reshape(2 * frames, 12 * frames)
    length = jnp.sum(member * clip_len[None, :], axis=1)
    count = length.astype(F32) * float(band * n_bands * width * (chans // GROUPS))
    count = jnp.concatenate([count, count])[:, None]
    group = jnp.arange(chans) // (chans // GROUPS)
    group = (group[:, None] == group[None, :]).astype(F32)
    all_ids = jnp.arange(n_time * frames, dtype=jnp.int32)
    _, all_member, all_start = clip_tables(clip_len, all_ids)
    codes = jnp.sum(all_member * owner[None, :], axis=1) * SEQ_CAP + all_ids - all_start
    codes = codes.astype(jnp.int32)

    sums = channel_stats(feat)
    for bit in (1, 2, 4):
        sums = sums + swap(sums, "rows", bit)
    pair = jnp.concatenate([sums, swap(sums, "tm", 1)], axis=0)
    sums = jnp.concatenate([pair, shift(pair, "tm", 2), shift(pair, "tm", -2)], axis=0)

    cbias = conv_bias[None, :]
    projt = jnp.tile(proj, (1, 128 // latent_ch))
    pbias = jnp.tile(proj_bias, 128 // latent_ch)[None, :]
    block, part, early, affine = local_part(
        local_start, edges, feat, top, bot, conv_weight, sums, mask, count, group,
        gamma[None, :], beta[None, :], cbias, projt, pbias,
    )
    block, lat = past_part(
        local_start, edges, past_one, past_two, border, past_top, past_bot, feat, conv_weight,
        part, affine, cbias, projt, pbias, early, block,
    )
    shares = lax.all_to_all(lat, "tm", split_axis=0, concat_axis=0, tiled=True)
    placed = place(codes, shares.reshape(n_time * frames, band, 128))
    seq = lax.all_to_all(
        placed.reshape(n_time, SEQ_CAP, band, 128), "tm", split_axis=0, concat_axis=0, tiled=True
    )
    return block, merge(seq)


def solution(mesh):
    in_specs = (P("tm", "rows", None, None), P(), P(), P(), P(), P(), P(), P(), P())
    out_specs = (P("tm", "rows", None, None), P("tm", "rows", None))
    return jax.shard_map(
        on_device, mesh=mesh, in_specs=in_specs, out_specs=out_specs, check_vma=False
    )
```

```python
import jax
import jax.numpy as jnp
from jax import lax
from jax.experimental import pallas as pl
from jax.experimental.pallas import tpu as pltpu
from jax.sharding import PartitionSpec as P

GROUPS = 32
SEQ_CAP = 8
CLIPS = 16
NH = 128
LOW = 1000
F32 = jnp.float32
BF16 = jnp.bfloat16
MIB = 2**20
STARTS, ENDS, EDGES, CODES = 0, 4, 8, 16
ANY = pl.BlockSpec(memory_space=pl.ANY)
VM = pl.BlockSpec(memory_space=pltpu.VMEM)
SM = pl.BlockSpec(memory_space=pltpu.SMEM)


def stats_kernel(ints, feat, o_ref, table, edge_ref, past_ref, x_ref, sums, sems, osems):
    frames, band = x_ref.shape[:2]
    quarter = band // 4
    loads = [
        pltpu.make_async_copy(
            feat.at[i // 4, pl.ds((i % 4) * quarter, quarter)],
            x_ref.at[i // 4, pl.ds((i % 4) * quarter, quarter)],
            sems.at[i],
        )
        for i in range(CLIPS)
    ]
    for c in loads:
        c.start()
    passes = [
        pltpu.make_async_copy(feat.at[f, row], edge_ref.at[side, f], osems.at[2 * f + side])
        for f in range(frames)
        for side, row in enumerate((band - 1, 0))
    ]
    passes.append(pltpu.make_async_copy(feat.at[pl.ds(2, 2)], past_ref, osems.at[2 * frames]))
    for c in passes:
        c.start()

    first = ints[0] * 4
    table[EDGES] = (ints[1] > 0).astype(jnp.int32)
    table[EDGES + 1] = (ints[1] < 7).astype(jnp.int32)
    starts = [jnp.int32(0)] * 4
    ends = [jnp.int32(0)] * 4
    start = jnp.int32(0)
    for i in range(CLIPS):
        end = start + ints[2 + i]
        base = ints[2 + CLIPS + i] * SEQ_CAP
        for own in range(4):
            inside = jnp.logical_and(first + own >= start, first + own < end)
            starts[own] = jnp.where(inside, start - first, starts[own])
            ends[own] = jnp.where(inside, end - first, ends[own])
        for k in range(SEQ_CAP):
            table[CODES + start + k] = base + k
        start = end
        loads[i].wait()
        f = i // 4
        x = x_ref[f, pl.ds((i % 4) * quarter, quarter)].astype(F32)
        x = x.reshape(-1, 8, x.shape[-1])
        one = jnp.sum(x, axis=0)
        two = jnp.sum(x * x, axis=0)
        if i % 4 == 0:
            sums[f] = one
            sums[4 + f] = two
        else:
            sums[f] += one
            sums[4 + f] += two
    for own in range(4):
        table[STARTS + own] = starts[own]
        table[ENDS + own] = ends[own]
    tot = jnp.sum(sums[...], axis=1)
    for d in range(o_ref.shape[0]):
        o_ref[d] = tot
    for c in passes:
        c.wait()


def channel_stats(ints, feat, copies):
    frames, band, width, chans = feat.shape
    return pl.pallas_call(
        stats_kernel,
        in_specs=[SM, ANY],
        out_specs=[VM, SM, ANY, ANY],
        out_shape=[
            jax.ShapeDtypeStruct((copies, 2 * frames, chans), F32),
            jax.ShapeDtypeStruct((CODES + 64 + SEQ_CAP,), jnp.int32),
            jax.ShapeDtypeStruct((2, frames, width, chans), BF16),
            jax.ShapeDtypeStruct((2, band, width, chans), BF16),
        ],
        scratch_shapes=[
            pltpu.VMEM(feat.shape, BF16),
            pltpu.VMEM((2 * frames, 8, chans), F32),
            pltpu.SemaphoreType.DMA((CLIPS,)),
            pltpu.SemaphoreType.DMA((2 * frames + 1,)),
        ],
        compiler_params=pltpu.CompilerParams(vmem_limit_bytes=16 * MIB),
        cost_estimate=pl.CostEstimate(flops=LOW, bytes_accessed=LOW, transcendentals=0),
        name="channel_stats",
    )(ints, pltpu.with_memory_space_constraint(feat, pltpu.HBM))


def clip_kernel(ints, table, sums, past_in, edge_in, o_ref, past, edge):
    del past_in, edge_in, past, edge
    shape = (8, sums.shape[0])
    row = lax.broadcasted_iota(jnp.int32, shape, 0)
    col = lax.broadcasted_iota(jnp.int32, shape, 1)
    frame = (col // 8) * 4 + col % 4 - 4 * ints[0]
    start = jnp.zeros(shape, jnp.int32)
    end = jnp.zeros(shape, jnp.int32)
    for f in range(4):
        start = jnp.where(row % 4 == f, table[STARTS + f], start)
        end = jnp.where(row % 4 == f, table[ENDS + f], end)
    inside = jnp.logical_and(frame >= start, frame < end)
    mask = jnp.where(jnp.logical_and(inside, row // 4 == (col // 4) % 2), 1.0, 0.0)
    tot = jnp.dot(mask, sums[...], precision=lax.Precision.HIGHEST, preferred_element_type=F32)
    for d in range(o_ref.shape[0]):
        o_ref[d] = tot


def clip_sums(ints, table, sums, past, edge, copies):
    return pl.pallas_call(
        clip_kernel,
        in_specs=[SM, SM, VM, ANY, ANY],
        out_specs=[VM, ANY, ANY],
        out_shape=[
            jax.ShapeDtypeStruct((copies, 8, sums.shape[1]), F32),
            jax.ShapeDtypeStruct(past.shape, BF16),
            jax.ShapeDtypeStruct(edge.shape, BF16),
        ],
        input_output_aliases={3: 1, 4: 2},
        compiler_params=pltpu.CompilerParams(vmem_limit_bytes=4 * MIB),
        cost_estimate=pl.CostEstimate(flops=LOW, bytes_accessed=LOW, transcendentals=0),
        name="clip_sums",
    )(ints, table, sums, past, edge)


def sides_kernel(near, top, bot, sides, sem):
    del near
    copies = [
        pltpu.make_async_copy(src.at[pl.ds(2, 2)], sides.at[k], sem.at[k])
        for k, src in enumerate((top, bot))
    ]
    for c in copies:
        c.start()
    for c in copies:
        c.wait()


def pack_sides(near, top, bot):
    return pl.pallas_call(
        sides_kernel,
        in_specs=[ANY] * 3,
        out_specs=ANY,
        out_shape=jax.ShapeDtypeStruct((2, 2) + top.shape[1:], BF16),
        scratch_shapes=[pltpu.SemaphoreType.DMA((2,))],
        compiler_params=pltpu.CompilerParams(vmem_limit_bytes=4 * MIB),
        cost_estimate=pl.CostEstimate(flops=LOW, bytes_accessed=LOW, transcendentals=0),
        name="pack_sides",
    )(near, top, bot)


def normed_rows(x, half_scale, half_shift):
    u = x.astype(F32) * half_scale + half_shift
    return u + u * jnp.tanh(u)


def put_rows(slab, row, h):
    width, chans = h.shape
    col = lax.broadcasted_iota(jnp.int32, h.shape, 0)
    left = jnp.where(col == 0, 0.0, pltpu.roll(h, 1, 0))
    right = jnp.where(col == width - 1, 0.0, pltpu.roll(h, width - 1, 0))
    slab[row, :, 0:chans] = left.astype(BF16)
    slab[row, :, chans : 2 * chans] = h.astype(BF16)
    slab[row, :, 2 * chans :] = right.astype(BF16)


def tap_dots(total, slab, weights, row, rows):
    for tap_row in range(3):
        lhs = slab[pl.ds(row + tap_row, rows)]
        lhs = lhs.reshape(rows * lhs.shape[1], lhs.shape[2])
        total = total + jnp.dot(lhs, weights[tap_row], preferred_element_type=F32)
    return total


def spread_latent(proj_ref, pbias_ref, projt, pbias):
    latent_ch, wide = proj_ref.shape[0], projt.shape[1]
    z = lax.broadcasted_iota(jnp.int32, (latent_ch, wide), 0)
    lane = lax.broadcasted_iota(jnp.int32, (latent_ch, wide), 1)
    spread = (lane % latent_ch == z).astype(F32)
    projt[...] = lax.dot_general(
        proj_ref[...], spread.astype(BF16), (((0,), (0,)), ((), ())), preferred_element_type=F32
    ).astype(BF16)
    pbias[...] = jnp.dot(
        pbias_ref[...], spread, precision=lax.Precision.HIGHEST, preferred_element_type=F32
    )


def latent_frame(block, projt, pbias, lscr, lat_ref, f):
    rows, width, chans = block.shape
    wide = projt.shape[1]
    per = wide // 16
    both = jnp.dot(
        block.reshape(rows * width, chans), projt[...], preferred_element_type=F32
    ).reshape(rows, width, wide)
    col = lax.broadcasted_iota(jnp.int32, both.shape, 1)
    lane = lax.broadcasted_iota(jnp.int32, both.shape, 2)
    lscr[...] = jnp.where(col % per == lane // 16, both, 0.0)
    for j in range(width // per):
        part = jnp.sum(lscr[:, per * j : per * (j + 1), :], axis=1) + pbias[...]
        lat_ref[j, f] = part.astype(BF16)


def local_kernel(
    table, feat, top, bot, w, near, gamma_ref, beta_ref, cbias_ref, proj_ref, pbias_ref,
    block_hbm, part, lat_ref, affine_ref,
    slab, obuf, lscr, projt, pbias, osems,
):
    tot = jnp.sum(near[...], axis=0)
    chans = tot.shape[1]
    per = chans // GROUPS
    group = (
        lax.broadcasted_iota(jnp.int32, (chans, chans), 0) // per
        == lax.broadcasted_iota(jnp.int32, (chans, chans), 1) // per
    ).astype(F32)
    tot = jnp.dot(tot, group, precision=lax.Precision.HIGHEST, preferred_element_type=F32)
    for f in range(4):
        count = ((table[ENDS + f] - table[STARTS + f]) * (NH * feat.shape[2] * per)).astype(F32)
        mean = tot[f : f + 1] / count
        var = tot[4 + f : 5 + f] / count - mean * mean
        scale = lax.rsqrt(var + 1e-06) * gamma_ref[...]
        affine_ref[f : f + 1] = 0.5 * scale
        affine_ref[4 + f : 5 + f] = 0.5 * (beta_ref[...] - mean * scale)
    spread_latent(proj_ref, pbias_ref, projt, pbias)

    starts = [table[STARTS + f] for f in range(4)]
    top_on = table[EDGES].astype(F32)
    bot_on = table[EDGES + 1].astype(F32)
    for f in range(4):
        hs = affine_ref[f : f + 1]
        hb = affine_ref[4 + f : 5 + f]
        page = slab.at[f]
        put_rows(page, 0, normed_rows(top[f], hs, hb) * top_on)
        put_rows(page, 17, normed_rows(bot[f], hs, hb) * bot_on)

        def norm_row(r, _, f=f, hs=hs, hb=hb, page=page):
            put_rows(page, r + 1, normed_rows(feat[f, r], hs, hb))
            return 0

        lax.fori_loop(0, 16, norm_row, 0, unroll=2)

    rows = 8
    zero = jnp.zeros((rows * 128, 256), F32)
    outs = []
    for f in (3, 2):
        src = [jnp.maximum(f - 2 + a, starts[f]) for a in range(3)]

        def chunk(m, _, f=f, src=src):
            total = zero
            for a in range(3):
                total = tap_dots(total, slab.at[src[a]], w.at[a], m * rows, rows)
            total = total.reshape(rows, 128, 256)
            r = pl.ds(m * rows, rows)
            obuf[f - 2, r] = (total + feat[f, r].astype(F32) + cbias_ref[...]).astype(BF16)
            return 0

        lax.fori_loop(0, 2, chunk, 0)
        c = pltpu.make_async_copy(obuf.at[f - 2], block_hbm.at[f], osems.at[f - 2])
        c.start()
        outs.append(c)
        latent_frame(obuf[f - 2], projt, pbias, lscr, lat_ref, f - 2)

    src1 = jnp.maximum(0, starts[1])

    def chunk1(m, _):
        total = tap_dots(zero, slab.at[1], w.at[2], m * rows, rows)
        total = tap_dots(total, slab.at[src1], w.at[1], m * rows, rows)
        part[1, pl.ds(m * rows, rows)] = total.reshape(rows, 128, 256)
        return 0

    lax.fori_loop(0, 2, chunk1, 0)

    def chunk0(m, _):
        total = tap_dots(zero, slab.at[0], w.at[2], m * rows, rows)
        part[0, pl.ds(m * rows, rows)] = total.reshape(rows, 128, 256)
        return 0

    lax.fori_loop(0, 2, chunk0, 0)

    @pl.when(starts[1] >= 0)
    def _():
        def more(m, _):
            r = pl.ds(m * rows, rows)
            total = part[1, r].reshape(rows * 128, 256)
            total = tap_dots(total, slab.at[src1], w.at[0], m * rows, rows)
            part[1, r] = total.reshape(rows, 128, 256)
            return 0

        lax.fori_loop(0, 2, more, 0)

    @pl.when(starts[0] >= 0)
    def _():
        def more(m, _):
            r = pl.ds(m * rows, rows)
            total = part[0, r].reshape(rows * 128, 256)
            total = tap_dots(total, slab.at[0], w.at[0], m * rows, rows)
            total = tap_dots(total, slab.at[0], w.at[1], m * rows, rows)
            part[0, r] = total.reshape(rows, 128, 256)
            return 0

        lax.fori_loop(0, 2, more, 0)

    for c in outs:
        c.wait()


def local_part(table, feat, top, bot, weight, near, gamma, beta, cbias, proj, pbias):
    shape = feat.shape
    return pl.pallas_call(
        local_kernel,
        in_specs=[SM] + [VM] * 10,
        out_specs=[ANY, VM, VM, VM],
        out_shape=[
            jax.ShapeDtypeStruct(shape, BF16),
            jax.ShapeDtypeStruct((2,) + shape[1:], F32),
            jax.ShapeDtypeStruct((16, 2, 16, 128), BF16),
            jax.ShapeDtypeStruct((8, 256), F32),
        ],
        scratch_shapes=[
            pltpu.VMEM((4, 18, 128, 768), BF16),
            pltpu.VMEM((2, 16, 128, 256), BF16),
            pltpu.VMEM((16, 128, 128), F32),
            pltpu.VMEM((256, 128), BF16),
            pltpu.VMEM((1, 128), F32),
            pltpu.SemaphoreType.DMA((2,)),
        ],
        compiler_params=pltpu.CompilerParams(vmem_limit_bytes=36 * MIB),
        cost_estimate=pl.CostEstimate(flops=LOW, bytes_accessed=LOW, transcendentals=0),
        name="local_conv",
    )(table, feat, top, bot, weight, near, gamma, beta, cbias, proj, pbias)


def past_kernel(
    table, past, sides, feat, w, part_in, affine_ref, cbias_ref, proj_ref, pbias_ref, early_ref,
    block_in,
    block_hbm, lat_ref,
    slab, obuf, part, lscr, projt, pbias, osems,
):
    del block_in
    spread_latent(proj_ref, pbias_ref, projt, pbias)
    starts = [table[STARTS + f] for f in range(2)]
    top_on = table[EDGES].astype(F32)
    bot_on = table[EDGES + 1].astype(F32)
    hs = affine_ref[0:1]
    hb = affine_ref[4:5]
    for p in range(2):
        @pl.when(starts[0] < p - 1)
        def _(p=p):
            page = slab.at[p]
            put_rows(page, 0, normed_rows(sides[0, p], hs, hb) * top_on)
            put_rows(page, 17, normed_rows(sides[1, p], hs, hb) * bot_on)

            def norm_row(r, _):
                put_rows(page, r + 1, normed_rows(past[p, r], hs, hb))
                return 0

            lax.fori_loop(0, 16, norm_row, 0, unroll=2)
    part[...] = part_in[...]
    rows = 8

    @pl.when(starts[1] < 0)
    def _():
        def more(m, _):
            r = pl.ds(m * rows, rows)
            total = part[1, r].reshape(rows * 128, 256)
            total = tap_dots(total, slab.at[1], w.at[0], m * rows, rows)
            part[1, r] = total.reshape(rows, 128, 256)
            return 0

        lax.fori_loop(0, 2, more, 0)

    src0 = jnp.clip(starts[0] + 2, 0, 1)

    @pl.when(starts[0] < 0)
    def _():
        def more(m, _):
            r = pl.ds(m * rows, rows)
            total = part[0, r].reshape(rows * 128, 256)
            total = tap_dots(total, slab.at[1], w.at[1], m * rows, rows)
            total = tap_dots(total, slab.at[src0], w.at[0], m * rows, rows)
            part[0, r] = total.reshape(rows, 128, 256)
            return 0

        lax.fori_loop(0, 2, more, 0)

    outs = []
    for f in (1, 0):
        def finish(r, _, f=f):
            rr = pl.ds(r * 2, 2)
            obuf[f, rr] = (part[f, rr] + feat[f, rr].astype(F32) + cbias_ref[...]).astype(BF16)
            return 0

        lax.fori_loop(0, 8, finish, 0)
        c = pltpu.make_async_copy(obuf.at[f], block_hbm.at[f], osems.at[f])
        c.start()
        outs.append(c)
        latent_frame(obuf[f], projt, pbias, lscr, lat_ref, f)
    lat_ref[:, 2:4] = early_ref[...]
    for c in outs:
        c.wait()


def past_part(table, past, sides, feat, weight, part, affine, cbias, proj, pbias, early, block):
    shape = feat.shape
    head = pl.BlockSpec((2,) + shape[1:], lambda i: (0, 0, 0, 0))
    return pl.pallas_call(
        past_kernel,
        grid=(1,),
        in_specs=[SM, VM, VM, head, pl.BlockSpec((2,) + weight.shape[1:], lambda i: (0, 0, 0, 0))]
        + [VM] * 6
        + [ANY],
        out_specs=[ANY, VM],
        out_shape=[
            jax.ShapeDtypeStruct(shape, BF16),
            jax.ShapeDtypeStruct((16, 4, 16, 128), BF16),
        ],
        input_output_aliases={11: 0},
        scratch_shapes=[
            pltpu.VMEM((2, 18, 128, 768), BF16),
            pltpu.VMEM((2, 16, 128, 256), BF16),
            pltpu.VMEM((2, 16, 128, 256), F32),
            pltpu.VMEM((16, 128, 128), F32),
            pltpu.VMEM((256, 128), BF16),
            pltpu.VMEM((1, 128), F32),
            pltpu.SemaphoreType.DMA((2,)),
        ],
        compiler_params=pltpu.CompilerParams(vmem_limit_bytes=36 * MIB),
        cost_estimate=pl.CostEstimate(flops=LOW, bytes_accessed=LOW, transcendentals=0),
        name="past_conv",
    )(table, past, sides, feat, weight, part, affine, cbias, proj, pbias, early, block)


def place_kernel(table, x_ref, o_ref):
    o_ref[...] = jnp.zeros_like(o_ref)

    def put(t, _):
        o_ref[table[CODES + t]] = x_ref[t]
        return 0

    lax.fori_loop(0, x_ref.shape[0], put, 0, unroll=8)


def place(table, shares):
    return pl.pallas_call(
        place_kernel,
        in_specs=[SM, VM],
        out_specs=VM,
        out_shape=jax.ShapeDtypeStruct((128, 16, 128), BF16),
        compiler_params=pltpu.CompilerParams(vmem_limit_bytes=4 * MIB),
        name="place_frames",
    )(table, shares)


def merge_kernel(x_ref, o_ref):
    for j in range(x_ref.shape[0]):
        o_ref[:, :, 128 * j : 128 * (j + 1)] = x_ref[j]


def merge(seq):
    return pl.pallas_call(
        merge_kernel,
        in_specs=[VM],
        out_specs=VM,
        out_shape=jax.ShapeDtypeStruct((8, 16, 2048), BF16),
        compiler_params=pltpu.CompilerParams(vmem_limit_bytes=4 * MIB),
        name="merge_columns",
    )(seq)


def shift(x, axis, by):
    n = lax.axis_size(axis)
    return lax.ppermute(x, axis, [(i, i + by) for i in range(n) if 0 <= i + by < n])


def on_device(feat, gamma, beta, conv_weight, conv_bias, proj, proj_bias, clip_len, owner):
    frames, band = feat.shape[:2]
    n_time = lax.axis_size("tm")

    place_of = jnp.stack([lax.axis_index("tm"), lax.axis_index("rows")]).astype(jnp.int32)
    ints = jnp.concatenate([place_of, clip_len, owner])
    sums, table, edge, past = channel_stats(ints, feat, n_time)
    sums = lax.all_to_all(sums, "tm", split_axis=0, concat_axis=0, tiled=True)
    sums, past, edge = clip_sums(
        ints, table, sums.reshape(-1, sums.shape[-1]), past, edge, lax.axis_size("rows")
    )
    past = shift(past, "tm", 1)
    top, bot = shift(edge[0], "rows", 1), shift(edge[1], "rows", -1)
    near = lax.all_to_all(sums, "rows", split_axis=0, concat_axis=0, tiled=True)
    sides = shift(pack_sides(near, top, bot), "tm", 1)

    cbias, pbias = conv_bias[None, :], proj_bias[None, :]
    block, part, early, affine = local_part(
        table, feat, top, bot, conv_weight, near, gamma[None, :], beta[None, :], cbias, proj.T,
        pbias,
    )
    block, lat = past_part(
        table, past, sides, feat, conv_weight, part, affine, cbias, proj.T, pbias, early, block
    )
    shares = lax.all_to_all(lat, "tm", split_axis=0, concat_axis=0, tiled=True)
    placed = place(table, shares.reshape(n_time * frames, band, 128))
    seq = lax.all_to_all(
        placed.reshape(n_time, SEQ_CAP, band, 128), "tm", split_axis=0, concat_axis=0, tiled=True
    )
    return block, merge(seq)


def solution(mesh):
    in_specs = (P("tm", "rows", None, None), P(), P(), P(), P(), P(), P(), P(), P())
    out_specs = (P("tm", "rows", None, None), P("tm", "rows", None))
    return jax.shard_map(
        on_device, mesh=mesh, in_specs=in_specs, out_specs=out_specs, check_vma=False
    )
```

```python
import functools

import jax
import jax.numpy as jnp
from jax import lax
from jax.experimental import pallas as pl
from jax.experimental.pallas import tpu as pltpu
from jax.sharding import PartitionSpec as P

GROUPS = 32
SEQ_CAP = 8
CLIPS = 16
NH = 128
LOW = 1000
LOCAL_VMEM = 35
PAST_VMEM = 26
LATE = 7
AHEAD = 3
F32 = jnp.float32
BF16 = jnp.bfloat16
MIB = 2**20
STARTS, ENDS, EDGES, CODES = 0, 4, 8, 16
ANY = pl.BlockSpec(memory_space=pl.ANY)
VM = pl.BlockSpec(memory_space=pltpu.VMEM)
SM = pl.BlockSpec(memory_space=pltpu.SMEM)
HBM = pl.BlockSpec(memory_space=pltpu.HBM)


def stats_kernel(ints, feat, o_ref, table, edge_ref, one_ref, mid_ref, two_ref, x_ref, sums, sems, osems):
    frames, band = x_ref.shape[:2]
    quarter = band // 4
    loads = [
        pltpu.make_async_copy(
            feat.at[i // 4, pl.ds((i % 4) * quarter, quarter)],
            x_ref.at[i // 4, pl.ds((i % 4) * quarter, quarter)],
            sems.at[i],
        )
        for i in range(CLIPS)
    ]
    for c in loads:
        c.start()
    passes = [
        pltpu.make_async_copy(feat.at[f, row], edge_ref.at[side, f], osems.at[2 * f + side])
        for f in range(frames)
        for side, row in enumerate((band - 1, 0))
    ]
    split = band - AHEAD
    for i, (src, dst) in enumerate((
        (feat.at[3], one_ref.at[pl.ds(AHEAD, band)]),
        (feat.at[2, pl.ds(split, AHEAD)], one_ref.at[pl.ds(0, AHEAD)]),
        (feat.at[2, pl.ds(LATE, split - LATE)], mid_ref),
        (feat.at[2, pl.ds(0, LATE)], two_ref),
    )):
        passes.append(pltpu.make_async_copy(src, dst, osems.at[2 * frames + i]))
    for c in passes:
        c.start()

    first = ints[0] * 4
    table[EDGES] = (ints[1] > 0).astype(jnp.int32)
    table[EDGES + 1] = (ints[1] < 7).astype(jnp.int32)
    starts = [jnp.int32(0)] * 4
    ends = [jnp.int32(0)] * 4
    start = jnp.int32(0)
    for i in range(CLIPS):
        end = start + ints[2 + i]
        base = ints[2 + CLIPS + i] * SEQ_CAP
        for own in range(4):
            inside = jnp.logical_and(first + own >= start, first + own < end)
            starts[own] = jnp.where(inside, start - first, starts[own])
            ends[own] = jnp.where(inside, end - first, ends[own])
        for k in range(SEQ_CAP):
            table[CODES + start + k] = base + k
        start = end
        loads[i].wait()
        f = i // 4
        x = x_ref[f, pl.ds((i % 4) * quarter, quarter)].astype(F32)
        x = x.reshape(-1, 8, x.shape[-1])
        one = jnp.sum(x, axis=0)
        two = jnp.sum(x * x, axis=0)
        if i % 4 == 0:
            sums[f] = one
            sums[4 + f] = two
        else:
            sums[f] += one
            sums[4 + f] += two
    for own in range(4):
        table[STARTS + own] = starts[own]
        table[ENDS + own] = ends[own]
    tot = jnp.sum(sums[...], axis=1)
    for d in range(o_ref.shape[0]):
        o_ref[d] = tot
    for c in passes:
        c.wait()


def channel_stats(ints, feat, copies):
    frames, band, width, chans = feat.shape
    return pl.pallas_call(
        stats_kernel,
        in_specs=[SM, ANY],
        out_specs=[VM, SM, ANY, HBM, HBM, HBM],
        out_shape=[
            jax.ShapeDtypeStruct((copies, 2 * frames, chans), F32),
            jax.ShapeDtypeStruct((CODES + 64 + SEQ_CAP,), jnp.int32),
            jax.ShapeDtypeStruct((2, frames, width, chans), BF16),
            jax.ShapeDtypeStruct((band + AHEAD, width, chans), BF16),
            jax.ShapeDtypeStruct((band - AHEAD - LATE, width, chans), BF16),
            jax.ShapeDtypeStruct((LATE, width, chans), BF16),
        ],
        scratch_shapes=[
            pltpu.VMEM(feat.shape, BF16),
            pltpu.VMEM((2 * frames, 8, chans), F32),
            pltpu.SemaphoreType.DMA((CLIPS,)),
            pltpu.SemaphoreType.DMA((2 * frames + 4,)),
        ],
        compiler_params=pltpu.CompilerParams(vmem_limit_bytes=16 * MIB),
        cost_estimate=pl.CostEstimate(flops=LOW, bytes_accessed=LOW, transcendentals=0),
        name="channel_stats",
    )(ints, pltpu.with_memory_space_constraint(feat, pltpu.HBM))


def clip_kernel(ints, table, sums, past_in, edge_in, o_ref, past, edge):
    del past_in, edge_in, past, edge
    shape = (8, sums.shape[0])
    row = lax.broadcasted_iota(jnp.int32, shape, 0)
    col = lax.broadcasted_iota(jnp.int32, shape, 1)
    frame = (col // 8) * 4 + col % 4 - 4 * ints[0]
    start = jnp.zeros(shape, jnp.int32)
    end = jnp.zeros(shape, jnp.int32)
    for f in range(4):
        start = jnp.where(row % 4 == f, table[STARTS + f], start)
        end = jnp.where(row % 4 == f, table[ENDS + f], end)
    inside = jnp.logical_and(frame >= start, frame < end)
    mask = jnp.where(jnp.logical_and(inside, row // 4 == (col // 4) % 2), 1.0, 0.0)
    tot = jnp.dot(mask, sums[...], precision=lax.Precision.HIGHEST, preferred_element_type=F32)
    for d in range(o_ref.shape[0]):
        o_ref[d] = tot


def clip_sums(ints, table, sums, past, edge, copies):
    return pl.pallas_call(
        clip_kernel,
        in_specs=[SM, SM, VM, HBM, ANY],
        out_specs=[VM, HBM, ANY],
        out_shape=[
            jax.ShapeDtypeStruct((copies, 8, sums.shape[1]), F32),
            jax.ShapeDtypeStruct(past.shape, BF16),
            jax.ShapeDtypeStruct(edge.shape, BF16),
        ],
        input_output_aliases={3: 1, 4: 2},
        compiler_params=pltpu.CompilerParams(vmem_limit_bytes=4 * MIB),
        cost_estimate=pl.CostEstimate(flops=LOW, bytes_accessed=LOW, transcendentals=0),
        name="clip_sums",
    )(ints, table, sums, past, edge)


def sides_kernel(near, top, bot, mid, sides, sem):
    del near
    copies = [
        pltpu.make_async_copy(src.at[2 + p], sides.at[2 * k + p], sem.at[2 * k + p])
        for k, src in enumerate((top, bot))
        for p in range(2)
    ]
    copies.append(pltpu.make_async_copy(mid, sides.at[pl.ds(4, mid.shape[0])], sem.at[4]))
    for c in copies:
        c.start()
    for c in copies:
        c.wait()


def pack_sides(near, top, bot, mid):
    return pl.pallas_call(
        sides_kernel,
        in_specs=[ANY] * 3 + [HBM],
        out_specs=ANY,
        out_shape=jax.ShapeDtypeStruct((4 + mid.shape[0],) + mid.shape[1:], BF16),
        scratch_shapes=[pltpu.SemaphoreType.DMA((5,))],
        compiler_params=pltpu.CompilerParams(vmem_limit_bytes=4 * MIB),
        cost_estimate=pl.CostEstimate(flops=LOW, bytes_accessed=LOW, transcendentals=0),
        name="pack_sides",
    )(near, top, bot, mid)


def normed_rows(x, half_scale, half_shift):
    u = x.astype(F32) * half_scale + half_shift
    return u + u * jnp.tanh(u)


def put_rows(slab, row, h):
    width, chans = h.shape
    col = lax.broadcasted_iota(jnp.int32, h.shape, 0)
    left = jnp.where(col == 0, 0.0, pltpu.roll(h, 1, 0))
    right = jnp.where(col == width - 1, 0.0, pltpu.roll(h, width - 1, 0))
    slab[row, :, 0:chans] = left.astype(BF16)
    slab[row, :, chans : 2 * chans] = h.astype(BF16)
    slab[row, :, 2 * chans :] = right.astype(BF16)


PAIRS = 8
UPPER, LOWER = range(0, 4), range(4, 8)
TAP0, TAP1, TAP2, TAP01, TAP012, NONE = 0, 1, 2, 3, 4, 5


def bank_kernel(w, sides, page_in, bank, page):
    del sides, page_in, page

    def step(i, _):
        r = pl.ds(pl.multiple_of(i * 16, 16), 16)
        taps = [[w[a, b, r].astype(F32) for b in range(3)] for a in range(3)]
        first = [x + y for x, y in zip(taps[0], taps[1])]
        taps += [first, [x + y for x, y in zip(first, taps[2])]]
        for n, (top, mid, low) in enumerate(taps):
            half = 0.5 * (top + low)
            mid = 0.5 * mid
            bank[4 * n, r] = top.astype(BF16)
            bank[4 * n + 1, r] = (half + mid).astype(BF16)
            bank[4 * n + 2, r] = (half - mid).astype(BF16)
            bank[4 * n + 3, r] = low.astype(BF16)
        bank[4 * NONE, r] = jnp.zeros(taps[0][0].shape, BF16)
        return 0

    lax.fori_loop(0, w.shape[2] // 16, step, 0)


def weight_bank(weight, sides, page):
    return pl.pallas_call(
        bank_kernel,
        in_specs=[VM, ANY, HBM],
        out_specs=[VM, HBM],
        out_shape=[
            jax.ShapeDtypeStruct((4 * NONE + 1,) + weight.shape[2:], BF16),
            jax.ShapeDtypeStruct(page.shape, BF16),
        ],
        input_output_aliases={2: 1},
        compiler_params=pltpu.CompilerParams(vmem_limit_bytes=16 * MIB),
        cost_estimate=pl.CostEstimate(flops=LOW, bytes_accessed=LOW, transcendentals=0),
        name="weight_bank",
    )(weight, sides, page)


def lift_steps(row, pairs, hs, hb, top_on, bot_on, page, lifted):
    ring = page.shape[0]
    first, last = 2 * pairs[0], 2 * pairs[-1] + 3

    def normed(r):
        h = normed_rows(row(r - 1), hs, hb)
        if r == 0:
            return h * top_on
        return h * bot_on if r == 2 * PAIRS + 1 else h

    def step(rows):
        for r in rows:
            put_rows(page, r % ring, normed(r))
            if r % 2 == 0 or r == first + 1:
                continue
            p = (r - 3) // 2
            d0, d1, d2, d3 = (page[(2 * p + k) % ring] for k in range(4))
            lifted[0, p] = d0 - d2
            lifted[1, p] = d1 + d2
            lifted[2, p] = d2 - d1
            lifted[3, p] = d3 - d1

    cuts = [first + (last + 1 - first) * i // 4 for i in range(5)]
    return [functools.partial(step, range(cuts[i], cuts[i + 1])) for i in range(4)]


def rows_of(raw, top, bot):
    return lambda r: top[...] if r < 0 else bot[...] if r == 2 * PAIRS else raw(r)


def product(bank, taps, k, pairs, total=None):
    for lifted, pick in taps:
        lhs = lifted[k, pairs[0] : pairs[-1] + 1]
        lhs = lhs.reshape(len(pairs) * lhs.shape[1], lhs.shape[2])
        rhs = bank[jnp.where(pick == NONE, 4 * NONE, 4 * pick + k)]
        d = jnp.dot(lhs, rhs, preferred_element_type=F32)
        total = d if total is None else total + d
    return total


def conv_frame(bank, taps, out, base, beside, pairs=range(PAIRS)):
    r = pl.ds(pairs[0], len(pairs))
    shape = (len(pairs),) + out.shape[2:]
    steps = list(beside) + [lambda: None] * 4
    m1 = product(bank, taps, 1, pairs)
    steps[0]()
    m2 = product(bank, taps, 2, pairs)
    steps[1]()
    even, odd = m1 + m2, m1 - m2
    if base is not None:
        even = even + base[0, r].reshape(even.shape)
        odd = odd + base[1, r].reshape(odd.shape)
    out[0, r] = product(bank, taps, 0, pairs, even).reshape(shape)
    steps[2]()
    out[1, r] = product(bank, taps, 3, pairs, odd).reshape(shape)
    steps[3]()


def pick_taps(start, t):
    return [
        jnp.where(start == t, TAP012, TAP2),
        jnp.where(start <= t - 2, TAP1, jnp.where(start == t - 1, TAP01, NONE)),
        jnp.where(start <= t - 2, TAP0, NONE),
    ]


def finish_steps(conv, feat, cbias_ref, obuf, pairs=range(PAIRS)):
    def step(some):
        for p in some:
            for q in range(2):
                r = 2 * p + q
                total = conv[q, p] + feat[r].astype(F32) + cbias_ref[...]
                obuf[r] = total.astype(BF16)

    n = len(pairs) // 4
    return [functools.partial(step, pairs[n * i : n * i + n]) for i in range(4)]


def spread_latent(proj_ref, pbias_ref, projt, pbias):
    latent_ch, wide = proj_ref.shape[0], projt.shape[1]
    z = lax.broadcasted_iota(jnp.int32, (latent_ch, wide), 0)
    lane = lax.broadcasted_iota(jnp.int32, (latent_ch, wide), 1)
    spread = (lane % latent_ch == z).astype(F32)
    projt[...] = lax.dot_general(
        proj_ref[...], spread.astype(BF16), (((0,), (0,)), ((), ())), preferred_element_type=F32
    ).astype(BF16)
    pbias[...] = jnp.dot(
        pbias_ref[...], spread, precision=lax.Precision.HIGHEST, preferred_element_type=F32
    )


def latent_frame(block, projt, pbias, lscr, lat_ref, f):
    rows, width, chans = block.shape
    wide = projt.shape[1]
    per = wide // 16
    both = jnp.dot(
        block.reshape(rows * width, chans), projt[...], preferred_element_type=F32
    ).reshape(rows, width, wide)
    col = lax.broadcasted_iota(jnp.int32, both.shape, 1)
    lane = lax.broadcasted_iota(jnp.int32, both.shape, 2)
    lscr[...] = jnp.where(col % per == lane // 16, both, 0.0)
    for j in range(width // per):
        part = jnp.sum(lscr[:, per * j : per * (j + 1), :], axis=1) + pbias[...]
        lat_ref[j, f] = part.astype(BF16)


def local_kernel(
    table, feat, top, bot, bank, near, gamma_ref, beta_ref, cbias_ref, proj_ref, pbias_ref,
    block_hbm, part, lat_ref, affine_ref,
    page, lift0, lift1, lift2, lift3, conv2, conv3, obuf, lscr, projt, pbias, osems,
):
    tot = jnp.sum(near[...], axis=0)
    chans = tot.shape[1]
    per = chans // GROUPS
    group = (
        lax.broadcasted_iota(jnp.int32, (chans, chans), 0) // per
        == lax.broadcasted_iota(jnp.int32, (chans, chans), 1) // per
    ).astype(F32)
    tot = jnp.dot(tot, group, precision=lax.Precision.HIGHEST, preferred_element_type=F32)
    for f in range(4):
        count = ((table[ENDS + f] - table[STARTS + f]) * (NH * feat.shape[2] * per)).astype(F32)
        mean = tot[f : f + 1] / count
        var = tot[4 + f : 5 + f] / count - mean * mean
        scale = lax.rsqrt(var + 1e-06) * gamma_ref[...]
        affine_ref[f : f + 1] = 0.5 * scale
        affine_ref[4 + f : 5 + f] = 0.5 * (beta_ref[...] - mean * scale)
    spread_latent(proj_ref, pbias_ref, projt, pbias)

    starts = [table[STARTS + f] for f in range(4)]
    top_on = table[EDGES].astype(F32)
    bot_on = table[EDGES + 1].astype(F32)
    lifts = (lift0, lift1, lift2, lift3)
    picks = [pick_taps(starts[t], t) for t in range(4)]

    def lift(f):
        return lift_steps(
            rows_of(lambda r: feat[f, r], top.at[f], bot.at[f]), range(PAIRS),
            affine_ref[f : f + 1], affine_ref[4 + f : 5 + f], top_on, bot_on, page, lifts[f],
        )

    def taps(t):
        return [(lifts[t - k], picks[t][k]) for k in range(min(t, 2) + 1)]

    def finish(f, conv):
        return finish_steps(conv, feat.at[f], cbias_ref, obuf.at[f - 2])

    def send(f):
        return pltpu.make_async_copy(obuf.at[f - 2], block_hbm.at[f], osems.at[f - 2])

    for step in lift(0):
        step()
    conv_frame(bank, taps(0), part.at[0], None, lift(1))
    conv_frame(bank, taps(1), part.at[1], None, lift(2))
    conv_frame(bank, taps(2), conv2, None, lift(3))
    conv_frame(bank, taps(3), conv3, None, finish(2, conv2))
    send(2).start()
    for step in finish(3, conv3):
        step()
    send(3).start()
    latent_frame(obuf[0], projt, pbias, lscr, lat_ref, 0)
    latent_frame(obuf[1], projt, pbias, lscr, lat_ref, 1)
    send(2).wait()
    send(3).wait()


def local_part(table, feat, top, bot, bank, near, gamma, beta, cbias, proj, pbias):
    shape = feat.shape
    return pl.pallas_call(
        local_kernel,
        in_specs=[SM] + [VM] * 10,
        out_specs=[ANY, VM, VM, VM],
        out_shape=[
            jax.ShapeDtypeStruct(shape, BF16),
            jax.ShapeDtypeStruct((2, 2, PAIRS) + shape[2:], F32),
            jax.ShapeDtypeStruct((16, 2, 16, 128), BF16),
            jax.ShapeDtypeStruct((8, 256), F32),
        ],
        scratch_shapes=[
            pltpu.VMEM((8, 128, 768), BF16),
            pltpu.VMEM((4, PAIRS, 128, 768), BF16),
            pltpu.VMEM((4, PAIRS, 128, 768), BF16),
            pltpu.VMEM((4, PAIRS, 128, 768), BF16),
            pltpu.VMEM((4, PAIRS, 128, 768), BF16),
            pltpu.VMEM((2, PAIRS, 128, 256), F32),
            pltpu.VMEM((2, PAIRS, 128, 256), F32),
            pltpu.VMEM((2, 16, 128, 256), BF16),
            pltpu.VMEM((16, 128, 128), F32),
            pltpu.VMEM((256, 128), BF16),
            pltpu.VMEM((1, 128), F32),
            pltpu.SemaphoreType.DMA((2,)),
        ],
        compiler_params=pltpu.CompilerParams(vmem_limit_bytes=LOCAL_VMEM * MIB),
        cost_estimate=pl.CostEstimate(flops=LOW, bytes_accessed=LOW, transcendentals=0),
        name="local_conv",
    )(table, feat, top, bot, bank, near, gamma, beta, cbias, proj, pbias)


def past_affine(table, affine_ref, p):
    on = table[STARTS] < -p
    return jnp.where(on, affine_ref[0:1], 0.0), jnp.where(on, affine_ref[4:5], 0.0)


def one_kernel(
    table, past, sides, feat, bank, part, affine_ref, cbias_ref, proj_ref, pbias_ref, block_in,
    block_hbm, half0, lat_ref,
    page, lift1, lift2, conv1, obuf, lscr, projt, pbias, sem,
):
    del block_in
    spread_latent(proj_ref, pbias_ref, projt, pbias)
    pick0, pick1 = pick_taps(table[STARTS], 0), pick_taps(table[STARTS + 1], 1)
    on = (table[EDGES].astype(F32), table[EDGES + 1].astype(F32))
    hs, hb = past_affine(table, affine_ref, 0)
    one = rows_of(lambda r: past[AHEAD + r], sides.at[1], sides.at[3])
    for step in lift_steps(one, range(PAIRS), hs, hb, *on, page, lift1):
        step()
    hs, hb = past_affine(table, affine_ref, 1)
    low = rows_of(lambda r: two_row(r, None, sides, past), None, sides.at[2])
    steps = lift_steps(low, LOWER, hs, hb, *on, page, lift2)
    conv_frame(bank, [(lift1, pick1[2])], conv1, part.at[1], steps)
    conv_frame(
        bank, [(lift1, pick0[1])], half0, part.at[0],
        finish_steps(conv1, feat.at[0], cbias_ref, obuf),
    )
    out = pltpu.make_async_copy(obuf, block_hbm.at[1], sem)
    out.start()
    conv_frame(bank, [(lift2, pick0[2])], half0, half0, [], LOWER)
    latent_frame(obuf[...], projt, pbias, lscr, lat_ref, 0)
    out.wait()


def two_row(r, late, sides, past):
    if r < LATE:
        return late[r]
    return sides[4 + r - LATE] if r < 2 * PAIRS - AHEAD else past[r - 2 * PAIRS + AHEAD]


def two_kernel(
    table, late, past, sides, feat, bank, half0, affine_ref, cbias_ref, proj_ref, pbias_ref,
    early_ref, one_ref, block_in,
    block_hbm, lat_ref,
    page, lifted, conv0, obuf, lscr, projt, pbias, sem,
):
    del block_in
    spread_latent(proj_ref, pbias_ref, projt, pbias)
    pick0 = pick_taps(table[STARTS], 0)
    on = (table[EDGES].astype(F32), table[EDGES + 1].astype(F32))
    hs, hb = past_affine(table, affine_ref, 1)
    rows = rows_of(lambda r: two_row(r, late, sides, past), sides.at[0], None)
    for step in lift_steps(rows, UPPER, hs, hb, *on, page, lifted):
        step()
    conv_frame(
        bank, [(lifted, pick0[2])], conv0, half0,
        finish_steps(half0, feat.at[0], cbias_ref, obuf, LOWER), UPPER,
    )
    for step in finish_steps(conv0, feat.at[0], cbias_ref, obuf, UPPER):
        step()
    out = pltpu.make_async_copy(obuf, block_hbm.at[0], sem)
    out.start()
    latent_frame(obuf[...], projt, pbias, lscr, lat_ref, 0)
    lat_ref[:, 1:2] = one_ref[...]
    lat_ref[:, 2:4] = early_ref[...]
    out.wait()


def past_scratch(shape, lifts):
    return [pltpu.VMEM((8, 128, 768), BF16)] + lifts * [
        pltpu.VMEM((4, PAIRS, 128, 768), BF16)
    ] + [
        pltpu.VMEM((2, PAIRS) + shape[2:], F32),
        pltpu.VMEM(shape[1:], BF16),
        pltpu.VMEM((16, 128, 128), F32),
        pltpu.VMEM((256, 128), BF16),
        pltpu.VMEM((1, 128), F32),
        pltpu.SemaphoreType.DMA,
    ]


def one_part(table, past, sides, feat, bank, part, affine, cbias, proj, pbias, block):
    shape = feat.shape
    return pl.pallas_call(
        one_kernel,
        grid=(1,),
        in_specs=[SM, VM, VM, pl.BlockSpec((1,) + shape[1:], lambda i: (1, 0, 0, 0))]
        + [VM] * 6
        + [ANY],
        out_specs=[ANY, VM, VM],
        out_shape=[
            jax.ShapeDtypeStruct(shape, BF16),
            jax.ShapeDtypeStruct(part.shape[1:], F32),
            jax.ShapeDtypeStruct((16, 1, 16, 128), BF16),
        ],
        input_output_aliases={10: 0},
        scratch_shapes=past_scratch(shape, 2),
        compiler_params=pltpu.CompilerParams(vmem_limit_bytes=PAST_VMEM * MIB),
        cost_estimate=pl.CostEstimate(flops=LOW, bytes_accessed=LOW, transcendentals=0),
        name="past_one",
    )(table, past, sides, feat, bank, part, affine, cbias, proj, pbias, block)


def two_part(
    table, late, past, sides, feat, bank, half0, affine, cbias, proj, pbias, early, one, block
):
    shape = feat.shape
    return pl.pallas_call(
        two_kernel,
        grid=(1,),
        in_specs=[SM, VM, VM, VM, pl.BlockSpec((1,) + shape[1:], lambda i: (0, 0, 0, 0))]
        + [VM] * 8
        + [ANY],
        out_specs=[ANY, VM],
        out_shape=[
            jax.ShapeDtypeStruct(shape, BF16),
            jax.ShapeDtypeStruct((16, 4, 16, 128), BF16),
        ],
        input_output_aliases={13: 0},
        scratch_shapes=past_scratch(shape, 1),
        compiler_params=pltpu.CompilerParams(vmem_limit_bytes=PAST_VMEM * MIB),
        cost_estimate=pl.CostEstimate(flops=LOW, bytes_accessed=LOW, transcendentals=0),
        name="past_two",
    )(table, late, past, sides, feat, bank, half0, affine, cbias, proj, pbias, early, one, block)


def place_kernel(table, x_ref, o_ref):
    o_ref[...] = jnp.zeros_like(o_ref)

    def put(t, _):
        o_ref[table[CODES + t]] = x_ref[t]
        return 0

    lax.fori_loop(0, x_ref.shape[0], put, 0, unroll=8)


def place(table, shares):
    return pl.pallas_call(
        place_kernel,
        in_specs=[SM, VM],
        out_specs=VM,
        out_shape=jax.ShapeDtypeStruct((128, 16, 128), BF16),
        compiler_params=pltpu.CompilerParams(vmem_limit_bytes=4 * MIB),
        name="place_frames",
    )(table, shares)


def merge_kernel(x_ref, o_ref):
    for j in range(x_ref.shape[0]):
        o_ref[:, :, 128 * j : 128 * (j + 1)] = x_ref[j]


def merge(seq):
    return pl.pallas_call(
        merge_kernel,
        in_specs=[VM],
        out_specs=VM,
        out_shape=jax.ShapeDtypeStruct((8, 16, 2048), BF16),
        compiler_params=pltpu.CompilerParams(vmem_limit_bytes=4 * MIB),
        name="merge_columns",
    )(seq)


def shift(x, axis, by):
    n = lax.axis_size(axis)
    return lax.ppermute(x, axis, [(i, i + by) for i in range(n) if 0 <= i + by < n])


def on_device(feat, gamma, beta, conv_weight, conv_bias, proj, proj_bias, clip_len, owner):
    frames, band = feat.shape[:2]
    n_time = lax.axis_size("tm")

    place_of = jnp.stack([lax.axis_index("tm"), lax.axis_index("rows")]).astype(jnp.int32)
    ints = jnp.concatenate([place_of, clip_len, owner])
    sums, table, edge, one, mid, two = channel_stats(ints, feat, n_time)
    sums = lax.all_to_all(sums, "tm", split_axis=0, concat_axis=0, tiled=True)
    sums, one, edge = clip_sums(
        ints, table, sums.reshape(-1, sums.shape[-1]), one, edge, lax.axis_size("rows")
    )
    one = shift(one, "tm", 1)
    top, bot = shift(edge[0], "rows", 1), shift(edge[1], "rows", -1)
    near = lax.all_to_all(sums, "rows", split_axis=0, concat_axis=0, tiled=True)
    sides = pack_sides(near, top, bot, mid)
    bank, two = weight_bank(conv_weight, sides, two)
    sides = shift(sides, "tm", 1)
    two = shift(two, "tm", 1)

    cbias, pbias = conv_bias[None, :], proj_bias[None, :]
    block, part, early, affine = local_part(
        table, feat, top, bot, bank, near, gamma[None, :], beta[None, :], cbias, proj.T,
        pbias,
    )
    block, part, lat = one_part(
        table, one, sides, feat, bank, part, affine, cbias, proj.T, pbias, block
    )
    block, lat = two_part(
        table, two, one, sides, feat, bank, part, affine, cbias, proj.T, pbias, early, lat, block
    )
    shares = lax.all_to_all(lat, "tm", split_axis=0, concat_axis=0, tiled=True)
    placed = place(table, shares.reshape(n_time * frames, band, 128))
    seq = lax.all_to_all(
        placed.reshape(n_time, SEQ_CAP, band, 128), "tm", split_axis=0, concat_axis=0, tiled=True
    )
    return block, merge(seq)


def solution(mesh):
    in_specs = (P("tm", "rows", None, None), P(), P(), P(), P(), P(), P(), P(), P())
    out_specs = (P("tm", "rows", None, None), P("tm", "rows", None))
    return jax.shard_map(
        on_device, mesh=mesh, in_specs=in_specs, out_specs=out_specs, check_vma=False
    )
```

```python
import functools

import jax
import jax.numpy as jnp
from jax import lax
from jax.experimental import pallas as pl
from jax.experimental.pallas import tpu as pltpu
from jax.sharding import PartitionSpec as P

GROUPS = 32
SEQ_CAP = 8
CLIPS = 16
NH = 128
LOW = 1000
LOCAL_VMEM = 35
PAST_VMEM = 26
LATE = 7
AHEAD = 3
F32 = jnp.float32
BF16 = jnp.bfloat16
MIB = 2**20
STARTS, ENDS, EDGES, FIRST, CODES = 0, 4, 8, 10, 16
ANY = pl.BlockSpec(memory_space=pl.ANY)
VM = pl.BlockSpec(memory_space=pltpu.VMEM)
SM = pl.BlockSpec(memory_space=pltpu.SMEM)
HBM = pl.BlockSpec(memory_space=pltpu.HBM)


def stats_kernel(
    clip_len_hbm, owner_hbm, feat, o_ref, table, down_ref, up_ref, one_ref, mid_ref, two_ref, x_ref, sums,
    clip_len, owner, sems, osems, isems,
):
    frames, band = x_ref.shape[:2]
    quarter = band // 4
    split = band - AHEAD
    ints = [
        pltpu.make_async_copy(clip_len_hbm, clip_len, isems.at[0]),
        pltpu.make_async_copy(owner_hbm, owner, isems.at[1]),
    ]
    for c in ints:
        c.start()
    order = [(f, q) for f in (2, 3, 0, 1) for q in range(4)]
    loads = [
        pltpu.make_async_copy(
            feat.at[f, pl.ds(q * quarter, quarter)],
            x_ref.at[f, pl.ds(q * quarter, quarter)],
            sems.at[i],
        )
        for i, (f, q) in enumerate(order)
    ]
    for c in loads:
        c.start()
    onward = {
        2: (
            (x_ref.at[2, pl.ds(split, AHEAD)], one_ref.at[pl.ds(0, AHEAD)]),
            (x_ref.at[2, pl.ds(LATE, split - LATE)], mid_ref),
            (x_ref.at[2, pl.ds(0, LATE)], two_ref),
        ),
        3: ((x_ref.at[3], one_ref.at[pl.ds(AHEAD, band)]),),
        0: (),
        1: (),
    }
    passes = []

    def send_on(src, dst):
        c = pltpu.make_async_copy(src, dst, osems.at[len(passes)])
        c.start()
        passes.append(c)

    first = lax.axis_index("tm") * 4
    row = lax.axis_index("rows")
    table[EDGES] = (row > 0).astype(jnp.int32)
    table[EDGES + 1] = (row < lax.axis_size("rows") - 1).astype(jnp.int32)
    table[FIRST] = first
    starts = [jnp.int32(0)] * 4
    ends = [jnp.int32(0)] * 4
    start = jnp.int32(0)
    for c in ints:
        c.wait()
    for i, (f, q) in enumerate(order):
        end = start + clip_len[i]
        base = owner[i] * SEQ_CAP
        for own in range(4):
            inside = jnp.logical_and(first + own >= start, first + own < end)
            starts[own] = jnp.where(inside, start - first, starts[own])
            ends[own] = jnp.where(inside, end - first, ends[own])
        for k in range(SEQ_CAP):
            table[CODES + start + k] = base + k
        start = end
        loads[i].wait()
        if q == 3:
            down_ref[f] = x_ref[f, band - 1]
            up_ref[f] = x_ref[f, 0]
            for src, dst in onward[f]:
                send_on(src, dst)
        x = x_ref[f, pl.ds(q * quarter, quarter)].astype(F32)
        x = x.reshape(-1, 8, x.shape[-1])
        one = jnp.sum(x, axis=0)
        two = jnp.sum(x * x, axis=0)
        if q == 0:
            sums[f] = one
            sums[4 + f] = two
        else:
            sums[f] += one
            sums[4 + f] += two
    for own in range(4):
        table[STARTS + own] = starts[own]
        table[ENDS + own] = ends[own]
    tot = jnp.sum(sums[...], axis=1)
    for d in range(o_ref.shape[0]):
        o_ref[d] = tot
    for c in passes:
        c.wait()


def channel_stats(clip_len, owner, feat, copies):
    frames, band, width, chans = feat.shape
    return pl.pallas_call(
        stats_kernel,
        in_specs=[HBM, HBM, HBM],
        out_specs=[VM, SM, VM, VM, HBM, HBM, HBM],
        out_shape=[
            jax.ShapeDtypeStruct((copies, 2 * frames, chans), F32),
            jax.ShapeDtypeStruct((CODES + 64 + SEQ_CAP,), jnp.int32),
            jax.ShapeDtypeStruct((frames, width, chans), BF16),
            jax.ShapeDtypeStruct((frames, width, chans), BF16),
            jax.ShapeDtypeStruct((band + AHEAD, width, chans), BF16),
            jax.ShapeDtypeStruct((band - AHEAD - LATE, width, chans), BF16),
            jax.ShapeDtypeStruct((LATE, width, chans), BF16),
        ],
        scratch_shapes=[
            pltpu.VMEM(feat.shape, BF16),
            pltpu.VMEM((2 * frames, 8, chans), F32),
            pltpu.SMEM((CLIPS,), jnp.int32),
            pltpu.SMEM((CLIPS,), jnp.int32),
            pltpu.SemaphoreType.DMA((CLIPS,)),
            pltpu.SemaphoreType.DMA((4,)),
            pltpu.SemaphoreType.DMA((2,)),
        ],
        compiler_params=pltpu.CompilerParams(vmem_limit_bytes=16 * MIB),
        cost_estimate=pl.CostEstimate(flops=LOW, bytes_accessed=LOW, transcendentals=0),
        name="channel_stats",
    )(*(pltpu.with_memory_space_constraint(x, pltpu.HBM) for x in (clip_len, owner, feat)))


def clip_kernel(table, sums, past_in, down_in, up_in, o_ref, past, down, up):
    del past_in, down_in, up_in, past, down, up
    shape = (8, sums.shape[0])
    row = lax.broadcasted_iota(jnp.int32, shape, 0)
    col = lax.broadcasted_iota(jnp.int32, shape, 1)
    frame = (col // 8) * 4 + col % 4 - table[FIRST]
    start = jnp.zeros(shape, jnp.int32)
    end = jnp.zeros(shape, jnp.int32)
    for f in range(4):
        start = jnp.where(row % 4 == f, table[STARTS + f], start)
        end = jnp.where(row % 4 == f, table[ENDS + f], end)
    inside = jnp.logical_and(frame >= start, frame < end)
    mask = jnp.where(jnp.logical_and(inside, row // 4 == (col // 4) % 2), 1.0, 0.0)
    tot = jnp.dot(mask, sums[...], precision=lax.Precision.HIGHEST, preferred_element_type=F32)
    for d in range(o_ref.shape[0]):
        o_ref[d] = tot


def clip_sums(table, sums, past, down, up, copies):
    return pl.pallas_call(
        clip_kernel,
        in_specs=[SM, VM, HBM, ANY, ANY],
        out_specs=[VM, HBM, ANY, ANY],
        out_shape=[
            jax.ShapeDtypeStruct((copies, 8, sums.shape[1]), F32),
            jax.ShapeDtypeStruct(past.shape, BF16),
            jax.ShapeDtypeStruct(down.shape, BF16),
            jax.ShapeDtypeStruct(up.shape, BF16),
        ],
        input_output_aliases={2: 1, 3: 2, 4: 3},
        compiler_params=pltpu.CompilerParams(vmem_limit_bytes=4 * MIB),
        cost_estimate=pl.CostEstimate(flops=LOW, bytes_accessed=LOW, transcendentals=0),
        name="clip_sums",
    )(table, sums, past, down, up)


def sides_kernel(near, top, bot, mid, sides, sem):
    del near
    copies = [
        pltpu.make_async_copy(src.at[2 + p], sides.at[2 * k + p], sem.at[2 * k + p])
        for k, src in enumerate((top, bot))
        for p in range(2)
    ]
    copies.append(pltpu.make_async_copy(mid, sides.at[pl.ds(4, mid.shape[0])], sem.at[4]))
    for c in copies:
        c.start()
    for c in copies:
        c.wait()


def pack_sides(near, top, bot, mid):
    return pl.pallas_call(
        sides_kernel,
        in_specs=[ANY] * 3 + [HBM],
        out_specs=ANY,
        out_shape=jax.ShapeDtypeStruct((4 + mid.shape[0],) + mid.shape[1:], BF16),
        scratch_shapes=[pltpu.SemaphoreType.DMA((5,))],
        compiler_params=pltpu.CompilerParams(vmem_limit_bytes=4 * MIB),
        cost_estimate=pl.CostEstimate(flops=LOW, bytes_accessed=LOW, transcendentals=0),
        name="pack_sides",
    )(near, top, bot, mid)


def normed_rows(x, half_scale, half_shift):
    u = x.astype(F32) * half_scale + half_shift
    return u + u * jnp.tanh(u)


def put_rows(slab, row, h):
    width, chans = h.shape
    col = lax.broadcasted_iota(jnp.int32, h.shape, 0)
    left = jnp.where(col == 0, 0.0, pltpu.roll(h, 1, 0))
    right = jnp.where(col == width - 1, 0.0, pltpu.roll(h, width - 1, 0))
    slab[row, :, 0:chans] = left.astype(BF16)
    slab[row, :, chans : 2 * chans] = h.astype(BF16)
    slab[row, :, 2 * chans :] = right.astype(BF16)


PAIRS = 8
UPPER, LOWER = range(0, 4), range(4, 8)
TAP0, TAP1, TAP2, TAP01, TAP012, NONE = 0, 1, 2, 3, 4, 5


def bank_kernel(w, sides, page_in, bank, page):
    del sides, page_in, page

    def step(i, _):
        r = pl.ds(pl.multiple_of(i * 16, 16), 16)
        taps = [[w[a, b, r].astype(F32) for b in range(3)] for a in range(3)]
        first = [x + y for x, y in zip(taps[0], taps[1])]
        taps += [first, [x + y for x, y in zip(first, taps[2])]]
        for n, (top, mid, low) in enumerate(taps):
            half = 0.5 * (top + low)
            mid = 0.5 * mid
            bank[4 * n, r] = top.astype(BF16)
            bank[4 * n + 1, r] = (half + mid).astype(BF16)
            bank[4 * n + 2, r] = (half - mid).astype(BF16)
            bank[4 * n + 3, r] = low.astype(BF16)
        bank[4 * NONE, r] = jnp.zeros(taps[0][0].shape, BF16)
        return 0

    lax.fori_loop(0, w.shape[2] // 16, step, 0)


def weight_bank(weight, sides, page):
    return pl.pallas_call(
        bank_kernel,
        in_specs=[VM, ANY, HBM],
        out_specs=[VM, HBM],
        out_shape=[
            jax.ShapeDtypeStruct((4 * NONE + 1,) + weight.shape[2:], BF16),
            jax.ShapeDtypeStruct(page.shape, BF16),
        ],
        input_output_aliases={2: 1},
        compiler_params=pltpu.CompilerParams(vmem_limit_bytes=16 * MIB),
        cost_estimate=pl.CostEstimate(flops=LOW, bytes_accessed=LOW, transcendentals=0),
        name="weight_bank",
    )(weight, sides, page)


def lift_steps(row, pairs, hs, hb, top_on, bot_on, page, lifted):
    ring = page.shape[0]
    first, last = 2 * pairs[0], 2 * pairs[-1] + 3

    def normed(r):
        h = normed_rows(row(r - 1), hs, hb)
        if r == 0:
            return h * top_on
        return h * bot_on if r == 2 * PAIRS + 1 else h

    def step(rows):
        for r in rows:
            put_rows(page, r % ring, normed(r))
            if r % 2 == 0 or r == first + 1:
                continue
            p = (r - 3) // 2
            d0, d1, d2, d3 = (page[(2 * p + k) % ring] for k in range(4))
            lifted[0, p] = d0 - d2
            lifted[1, p] = d1 + d2
            lifted[2, p] = d2 - d1
            lifted[3, p] = d3 - d1

    cuts = [first + (last + 1 - first) * i // 4 for i in range(5)]
    return [functools.partial(step, range(cuts[i], cuts[i + 1])) for i in range(4)]


def rows_of(raw, top, bot):
    return lambda r: top[...] if r < 0 else bot[...] if r == 2 * PAIRS else raw(r)


def product(bank, taps, k, pairs, total=None):
    for lifted, pick in taps:
        lhs = lifted[k, pairs[0] : pairs[-1] + 1]
        lhs = lhs.reshape(len(pairs) * lhs.shape[1], lhs.shape[2])
        rhs = bank[jnp.where(pick == NONE, 4 * NONE, 4 * pick + k)]
        d = jnp.dot(lhs, rhs, preferred_element_type=F32)
        total = d if total is None else total + d
    return total


def conv_frame(bank, taps, out, base, beside, pairs=range(PAIRS)):
    r = pl.ds(pairs[0], len(pairs))
    shape = (len(pairs),) + out.shape[2:]
    steps = list(beside) + [lambda: None] * 4
    m1 = product(bank, taps, 1, pairs)
    steps[0]()
    m2 = product(bank, taps, 2, pairs)
    steps[1]()
    even, odd = m1 + m2, m1 - m2
    if base is not None:
        even = even + base[0, r].reshape(even.shape)
        odd = odd + base[1, r].reshape(odd.shape)
    out[0, r] = product(bank, taps, 0, pairs, even).reshape(shape)
    steps[2]()
    out[1, r] = product(bank, taps, 3, pairs, odd).reshape(shape)
    steps[3]()


def pick_taps(start, t):
    return [
        jnp.where(start == t, TAP012, TAP2),
        jnp.where(start <= t - 2, TAP1, jnp.where(start == t - 1, TAP01, NONE)),
        jnp.where(start <= t - 2, TAP0, NONE),
    ]


def finish_steps(conv, feat, cbias_ref, obuf, pairs=range(PAIRS)):
    def step(some):
        for p in some:
            for q in range(2):
                r = 2 * p + q
                total = conv[q, p] + feat[r].astype(F32) + cbias_ref[...]
                obuf[r] = total.astype(BF16)

    n = len(pairs) // 4
    return [functools.partial(step, pairs[n * i : n * i + n]) for i in range(4)]


def spread_latent(proj_ref, pbias_ref, projt, pbias):
    latent_ch, wide = proj_ref.shape[0], projt.shape[1]
    z = lax.broadcasted_iota(jnp.int32, (latent_ch, wide), 0)
    lane = lax.broadcasted_iota(jnp.int32, (latent_ch, wide), 1)
    spread = (lane % latent_ch == z).astype(F32)
    projt[...] = lax.dot_general(
        proj_ref[...], spread.astype(BF16), (((0,), (0,)), ((), ())), preferred_element_type=F32
    ).astype(BF16)
    pbias[...] = jnp.dot(
        pbias_ref[...], spread, precision=lax.Precision.HIGHEST, preferred_element_type=F32
    )


def latent_frame(block, projt, pbias, lscr, lat_ref, f):
    rows, width, chans = block.shape
    wide = projt.shape[1]
    per = wide // 16
    both = jnp.dot(
        block.reshape(rows * width, chans), projt[...], preferred_element_type=F32
    ).reshape(rows, width, wide)
    col = lax.broadcasted_iota(jnp.int32, both.shape, 1)
    lane = lax.broadcasted_iota(jnp.int32, both.shape, 2)
    lscr[...] = jnp.where(col % per == lane // 16, both, 0.0)
    for j in range(width // per):
        part = jnp.sum(lscr[:, per * j : per * (j + 1), :], axis=1) + pbias[...]
        lat_ref[j, f] = part.astype(BF16)


def local_kernel(
    table, feat, top, bot, bank, near, gamma_ref, beta_ref, cbias_ref, proj_ref, pbias_ref,
    block_hbm, part, lat_ref, affine_ref, projt, pbias,
    page, lift0, lift1, lift2, lift3, conv2, conv3, obuf, lscr, osems,
):
    tot = jnp.sum(near[...], axis=0)
    chans = tot.shape[1]
    per = chans // GROUPS
    group = (
        lax.broadcasted_iota(jnp.int32, (chans, chans), 0) // per
        == lax.broadcasted_iota(jnp.int32, (chans, chans), 1) // per
    ).astype(F32)
    tot = jnp.dot(tot, group, precision=lax.Precision.HIGHEST, preferred_element_type=F32)
    for f in range(4):
        count = ((table[ENDS + f] - table[STARTS + f]) * (NH * feat.shape[2] * per)).astype(F32)
        mean = tot[f : f + 1] / count
        var = tot[4 + f : 5 + f] / count - mean * mean
        scale = lax.rsqrt(var + 1e-06) * gamma_ref[...]
        affine_ref[f : f + 1] = 0.5 * scale
        affine_ref[4 + f : 5 + f] = 0.5 * (beta_ref[...] - mean * scale)
    spread_latent(proj_ref, pbias_ref, projt, pbias)

    starts = [table[STARTS + f] for f in range(4)]
    top_on = table[EDGES].astype(F32)
    bot_on = table[EDGES + 1].astype(F32)
    lifts = (lift0, lift1, lift2, lift3)
    picks = [pick_taps(starts[t], t) for t in range(4)]

    def lift(f, pairs=range(PAIRS)):
        return lift_steps(
            rows_of(lambda r: feat[f, r], top.at[f], bot.at[f]), pairs,
            affine_ref[f : f + 1], affine_ref[4 + f : 5 + f], top_on, bot_on, page, lifts[f],
        )

    def taps(t):
        return [(lifts[t - k], picks[t][k]) for k in range(min(t, 2) + 1)]

    def finish(f, conv):
        return finish_steps(conv, feat.at[f], cbias_ref, obuf.at[f - 2])

    def send(f):
        return pltpu.make_async_copy(obuf.at[f - 2], block_hbm.at[f], osems.at[f - 2])

    for step in lift(0, UPPER):
        step()
    conv_frame(bank, taps(0), part.at[0], None, lift(0, LOWER), UPPER)
    conv_frame(bank, taps(0), part.at[0], None, lift(1), LOWER)
    conv_frame(bank, taps(1), part.at[1], None, lift(2))
    conv_frame(bank, taps(2), conv2, None, lift(3))
    conv_frame(bank, taps(3), conv3, None, finish(2, conv2))
    send(2).start()
    for step in finish(3, conv3):
        step()
    send(3).start()
    latent_frame(obuf[0], projt, pbias, lscr, lat_ref, 0)
    latent_frame(obuf[1], projt, pbias, lscr, lat_ref, 1)
    send(2).wait()
    send(3).wait()


def local_part(table, feat, top, bot, bank, near, gamma, beta, cbias, proj, pbias):
    shape = feat.shape
    return pl.pallas_call(
        local_kernel,
        in_specs=[SM] + [VM] * 10,
        out_specs=[ANY, VM, VM, VM, VM, VM],
        out_shape=[
            jax.ShapeDtypeStruct(shape, BF16),
            jax.ShapeDtypeStruct((2, 2, PAIRS) + shape[2:], F32),
            jax.ShapeDtypeStruct((16, 2, 16, 128), BF16),
            jax.ShapeDtypeStruct((8, 256), F32),
            jax.ShapeDtypeStruct((256, 128), BF16),
            jax.ShapeDtypeStruct((1, 128), F32),
        ],
        scratch_shapes=[
            pltpu.VMEM((8, 128, 768), BF16),
            pltpu.VMEM((4, PAIRS, 128, 768), BF16),
            pltpu.VMEM((4, PAIRS, 128, 768), BF16),
            pltpu.VMEM((4, PAIRS, 128, 768), BF16),
            pltpu.VMEM((4, PAIRS, 128, 768), BF16),
            pltpu.VMEM((2, PAIRS, 128, 256), F32),
            pltpu.VMEM((2, PAIRS, 128, 256), F32),
            pltpu.VMEM((2, 16, 128, 256), BF16),
            pltpu.VMEM((16, 128, 128), F32),
            pltpu.SemaphoreType.DMA((2,)),
        ],
        compiler_params=pltpu.CompilerParams(vmem_limit_bytes=LOCAL_VMEM * MIB),
        cost_estimate=pl.CostEstimate(flops=LOW, bytes_accessed=LOW, transcendentals=0),
        name="local_conv",
    )(table, feat, top, bot, bank, near, gamma, beta, cbias, proj, pbias)


def past_affine(table, affine_ref, p):
    on = table[STARTS] < -p
    return jnp.where(on, affine_ref[0:1], 0.0), jnp.where(on, affine_ref[4:5], 0.0)


def one_kernel(
    table, past, sides, feat, bank, part, affine_ref, cbias_ref, projt, pbias, block_in,
    block_hbm, half0, lat_ref,
    page, lift1, lift2, conv1, obuf, lscr, sem,
):
    del block_in
    pick0, pick1 = pick_taps(table[STARTS], 0), pick_taps(table[STARTS + 1], 1)
    on = (table[EDGES].astype(F32), table[EDGES + 1].astype(F32))
    hs, hb = past_affine(table, affine_ref, 0)
    one = rows_of(lambda r: past[AHEAD + r], sides.at[1], sides.at[3])
    for step in lift_steps(one, UPPER, hs, hb, *on, page, lift1):
        step()
    rest = lift_steps(one, LOWER, hs, hb, *on, page, lift1)
    hs, hb = past_affine(table, affine_ref, 1)
    low = rows_of(lambda r: two_row(r, None, sides, past), None, sides.at[2])
    steps = lift_steps(low, LOWER, hs, hb, *on, page, lift2)
    conv_frame(bank, [(lift1, pick1[2])], conv1, part.at[1], rest, UPPER)
    conv_frame(bank, [(lift1, pick1[2])], conv1, part.at[1], steps, LOWER)
    conv_frame(
        bank, [(lift1, pick0[1])], half0, part.at[0],
        finish_steps(conv1, feat.at[1], cbias_ref, obuf),
    )
    out = pltpu.make_async_copy(obuf, block_hbm.at[1], sem)
    out.start()
    conv_frame(bank, [(lift2, pick0[2])], half0, half0, [], LOWER)
    latent_frame(obuf[...], projt, pbias, lscr, lat_ref, 0)
    out.wait()


def two_row(r, late, sides, past):
    if r < LATE:
        return late[r]
    return sides[4 + r - LATE] if r < 2 * PAIRS - AHEAD else past[r - 2 * PAIRS + AHEAD]


def two_kernel(
    table, late, past, sides, feat, bank, half0, affine_ref, cbias_ref, projt, pbias,
    early_ref, one_ref, block_in,
    block_hbm, lat_ref,
    page, lifted, conv0, obuf, lscr, sem,
):
    del block_in
    pick0 = pick_taps(table[STARTS], 0)
    on = (table[EDGES].astype(F32), table[EDGES + 1].astype(F32))
    hs, hb = past_affine(table, affine_ref, 1)
    rows = rows_of(lambda r: two_row(r, late, sides, past), sides.at[0], None)
    for step in lift_steps(rows, UPPER, hs, hb, *on, page, lifted):
        step()
    conv_frame(
        bank, [(lifted, pick0[2])], conv0, half0,
        finish_steps(half0, feat.at[0], cbias_ref, obuf, LOWER), UPPER,
    )
    for step in finish_steps(conv0, feat.at[0], cbias_ref, obuf, UPPER):
        step()
    out = pltpu.make_async_copy(obuf, block_hbm.at[0], sem)
    out.start()
    latent_frame(obuf[...], projt, pbias, lscr, lat_ref, 0)
    lat_ref[:, 1:2] = one_ref[...]
    lat_ref[:, 2:4] = early_ref[...]
    out.wait()


def past_scratch(shape, lifts):
    return [pltpu.VMEM((8, 128, 768), BF16)] + lifts * [
        pltpu.VMEM((4, PAIRS, 128, 768), BF16)
    ] + [
        pltpu.VMEM((2, PAIRS) + shape[2:], F32),
        pltpu.VMEM(shape[1:], BF16),
        pltpu.VMEM((16, 128, 128), F32),
        pltpu.SemaphoreType.DMA,
    ]


def one_part(table, past, sides, feat, bank, part, affine, cbias, proj, pbias, block):
    shape = feat.shape
    return pl.pallas_call(
        one_kernel,
        in_specs=[SM] + [VM] * 9 + [ANY],
        out_specs=[ANY, VM, VM],
        out_shape=[
            jax.ShapeDtypeStruct(shape, BF16),
            jax.ShapeDtypeStruct(part.shape[1:], F32),
            jax.ShapeDtypeStruct((16, 1, 16, 128), BF16),
        ],
        input_output_aliases={10: 0},
        scratch_shapes=past_scratch(shape, 2),
        compiler_params=pltpu.CompilerParams(vmem_limit_bytes=PAST_VMEM * MIB),
        cost_estimate=pl.CostEstimate(flops=LOW, bytes_accessed=LOW, transcendentals=0),
        name="past_one",
    )(table, past, sides, feat, bank, part, affine, cbias, proj, pbias, block)


def two_part(
    table, late, past, sides, feat, bank, half0, affine, cbias, proj, pbias, early, one, block
):
    shape = feat.shape
    return pl.pallas_call(
        two_kernel,
        in_specs=[SM] + [VM] * 12 + [ANY],
        out_specs=[ANY, VM],
        out_shape=[
            jax.ShapeDtypeStruct(shape, BF16),
            jax.ShapeDtypeStruct((16, 4, 16, 128), BF16),
        ],
        input_output_aliases={13: 0},
        scratch_shapes=past_scratch(shape, 1),
        compiler_params=pltpu.CompilerParams(vmem_limit_bytes=PAST_VMEM * MIB),
        cost_estimate=pl.CostEstimate(flops=LOW, bytes_accessed=LOW, transcendentals=0),
        name="past_two",
    )(table, late, past, sides, feat, bank, half0, affine, cbias, proj, pbias, early, one, block)


def place_kernel(table, x_ref, o_ref):
    o_ref[...] = jnp.zeros_like(o_ref)

    def put(t, _):
        o_ref[table[CODES + t]] = x_ref[t]
        return 0

    lax.fori_loop(0, x_ref.shape[0], put, 0, unroll=8)


def place(table, shares):
    return pl.pallas_call(
        place_kernel,
        in_specs=[SM, VM],
        out_specs=VM,
        out_shape=jax.ShapeDtypeStruct((128, 16, 128), BF16),
        compiler_params=pltpu.CompilerParams(vmem_limit_bytes=4 * MIB),
        name="place_frames",
    )(table, shares)


def merge_kernel(x_ref, o_ref):
    for j in range(x_ref.shape[0]):
        o_ref[:, :, 128 * j : 128 * (j + 1)] = x_ref[j]


def merge(seq):
    return pl.pallas_call(
        merge_kernel,
        in_specs=[VM],
        out_specs=VM,
        out_shape=jax.ShapeDtypeStruct((8, 16, 2048), BF16),
        compiler_params=pltpu.CompilerParams(vmem_limit_bytes=4 * MIB),
        name="merge_columns",
    )(seq)


def shift(x, axis, by):
    n = lax.axis_size(axis)
    return lax.ppermute(x, axis, [(i, i + by) for i in range(n) if 0 <= i + by < n])


def on_device(feat, gamma, beta, conv_weight, conv_bias, proj, proj_bias, clip_len, owner):
    frames, band = feat.shape[:2]
    n_time = lax.axis_size("tm")

    sums, table, down, up, one, mid, two = channel_stats(clip_len, owner, feat, n_time)
    sums = lax.all_to_all(sums, "tm", split_axis=0, concat_axis=0, tiled=True)
    sums, one, down, up = clip_sums(
        table, sums.reshape(-1, sums.shape[-1]), one, down, up, lax.axis_size("rows")
    )
    one = shift(one, "tm", 1)
    top, bot = shift(down, "rows", 1), shift(up, "rows", -1)
    near = lax.all_to_all(sums, "rows", split_axis=0, concat_axis=0, tiled=True)
    sides = pack_sides(near, top, bot, mid)
    bank, two = weight_bank(conv_weight, sides, two)
    sides = shift(sides, "tm", 1)
    two = shift(two, "tm", 1)

    cbias, pbias = conv_bias[None, :], proj_bias[None, :]
    block, part, early, affine, projt, ptile = local_part(
        table, feat, top, bot, bank, near, gamma[None, :], beta[None, :], cbias, proj.T,
        pbias,
    )
    block, part, lat = one_part(
        table, one, sides, feat, bank, part, affine, cbias, projt, ptile, block
    )
    block, lat = two_part(
        table, two, one, sides, feat, bank, part, affine, cbias, projt, ptile, early, lat, block
    )
    shares = lax.all_to_all(lat, "tm", split_axis=0, concat_axis=0, tiled=True)
    placed = place(table, shares.reshape(n_time * frames, band, 128))
    seq = lax.all_to_all(
        placed.reshape(n_time, SEQ_CAP, band, 128), "tm", split_axis=0, concat_axis=0, tiled=True
    )
    return block, merge(seq)


def solution(mesh):
    in_specs = (P("tm", "rows", None, None), P(), P(), P(), P(), P(), P(), P(), P())
    out_specs = (P("tm", "rows", None, None), P("tm", "rows", None))
    return jax.shard_map(
        on_device, mesh=mesh, in_specs=in_specs, out_specs=out_specs, check_vma=False
    )
```

```python
import functools

import jax
import jax.numpy as jnp
from jax import lax
from jax.experimental import pallas as pl
from jax.experimental.pallas import tpu as pltpu
from jax.sharding import PartitionSpec as P

GROUPS = 32
SEQ_CAP = 8
CLIPS = 16
NH = 128
LOW = 1000
LOCAL_VMEM = 35
PAST_VMEM = 26
LATE = 7
AHEAD = 3
F32 = jnp.float32
BF16 = jnp.bfloat16
MIB = 2**20
STARTS, ENDS, EDGES, FIRST, TABLE = 0, 4, 8, 10, 16
ANY = pl.BlockSpec(memory_space=pl.ANY)
VM = pl.BlockSpec(memory_space=pltpu.VMEM)
SM = pl.BlockSpec(memory_space=pltpu.SMEM)
HBM = pl.BlockSpec(memory_space=pltpu.HBM)


def stats_kernel(
    clip_len_hbm, feat, o_ref, table, down_ref, up_ref, one_ref, mid_ref, two_ref, x_ref, sums,
    clip_len, sems, osems, isem,
):
    frames, band = x_ref.shape[:2]
    quarter = band // 4
    split = band - AHEAD
    ints = pltpu.make_async_copy(clip_len_hbm, clip_len, isem)
    ints.start()
    order = [(f, q) for f in (2, 3, 0, 1) for q in range(4)]
    loads = [
        pltpu.make_async_copy(
            feat.at[f, pl.ds(q * quarter, quarter)],
            x_ref.at[f, pl.ds(q * quarter, quarter)],
            sems.at[i],
        )
        for i, (f, q) in enumerate(order)
    ]
    for c in loads:
        c.start()
    onward = {
        2: (
            (x_ref.at[2, pl.ds(split, AHEAD)], one_ref.at[pl.ds(0, AHEAD)]),
            (x_ref.at[2, pl.ds(LATE, split - LATE)], mid_ref),
            (x_ref.at[2, pl.ds(0, LATE)], two_ref),
        ),
        3: ((x_ref.at[3], one_ref.at[pl.ds(AHEAD, band)]),),
        0: (),
        1: (),
    }
    passes = []

    def send_on(src, dst):
        c = pltpu.make_async_copy(src, dst, osems.at[len(passes)])
        c.start()
        passes.append(c)

    first = lax.axis_index("tm") * 4
    row = lax.axis_index("rows")
    table[EDGES] = (row > 0).astype(jnp.int32)
    table[EDGES + 1] = (row < lax.axis_size("rows") - 1).astype(jnp.int32)
    table[FIRST] = first
    starts = [jnp.int32(0)] * 4
    ends = [jnp.int32(0)] * 4
    start = jnp.int32(0)
    ints.wait()
    for i, (f, q) in enumerate(order):
        end = start + clip_len[i]
        for own in range(4):
            inside = jnp.logical_and(first + own >= start, first + own < end)
            starts[own] = jnp.where(inside, start - first, starts[own])
            ends[own] = jnp.where(inside, end - first, ends[own])
        start = end
        loads[i].wait()
        if q == 3:
            down_ref[f] = x_ref[f, band - 1]
            up_ref[f] = x_ref[f, 0]
            for src, dst in onward[f]:
                send_on(src, dst)
        x = x_ref[f, pl.ds(q * quarter, quarter)].astype(F32)
        x = x.reshape(-1, 8, x.shape[-1])
        one = jnp.sum(x, axis=0)
        two = jnp.sum(x * x, axis=0)
        if q == 0:
            sums[f] = one
            sums[4 + f] = two
        else:
            sums[f] += one
            sums[4 + f] += two
    for own in range(4):
        table[STARTS + own] = starts[own]
        table[ENDS + own] = ends[own]
    tot = jnp.sum(sums[...], axis=1)
    for d in range(o_ref.shape[0]):
        o_ref[d] = tot
    for c in passes:
        c.wait()


def channel_stats(clip_len, feat, copies):
    frames, band, width, chans = feat.shape
    return pl.pallas_call(
        stats_kernel,
        in_specs=[HBM, HBM],
        out_specs=[VM, SM, VM, VM, HBM, HBM, HBM],
        out_shape=[
            jax.ShapeDtypeStruct((copies, 2 * frames, chans), F32),
            jax.ShapeDtypeStruct((TABLE,), jnp.int32),
            jax.ShapeDtypeStruct((frames, width, chans), BF16),
            jax.ShapeDtypeStruct((frames, width, chans), BF16),
            jax.ShapeDtypeStruct((band + AHEAD, width, chans), BF16),
            jax.ShapeDtypeStruct((band - AHEAD - LATE, width, chans), BF16),
            jax.ShapeDtypeStruct((LATE, width, chans), BF16),
        ],
        scratch_shapes=[
            pltpu.VMEM(feat.shape, BF16),
            pltpu.VMEM((2 * frames, 8, chans), F32),
            pltpu.SMEM((CLIPS,), jnp.int32),
            pltpu.SemaphoreType.DMA((CLIPS,)),
            pltpu.SemaphoreType.DMA((4,)),
            pltpu.SemaphoreType.DMA,
        ],
        compiler_params=pltpu.CompilerParams(vmem_limit_bytes=16 * MIB),
        cost_estimate=pl.CostEstimate(flops=LOW, bytes_accessed=LOW, transcendentals=0),
        name="channel_stats",
    )(*(pltpu.with_memory_space_constraint(x, pltpu.HBM) for x in (clip_len, feat)))


def after_kernel(sums, page_in, page):
    del sums, page_in, page


def after(sums, page):
    return pl.pallas_call(
        after_kernel,
        in_specs=[ANY, HBM],
        out_specs=HBM,
        out_shape=jax.ShapeDtypeStruct(page.shape, BF16),
        input_output_aliases={1: 0},
        compiler_params=pltpu.CompilerParams(vmem_limit_bytes=4 * MIB),
        cost_estimate=pl.CostEstimate(flops=LOW, bytes_accessed=LOW, transcendentals=0),
        name="after_sums",
    )(sums, page)


def clip_kernel(table, sums, down_in, up_in, o_ref, down, up):
    del down_in, up_in, down, up
    shape = (8, sums.shape[0])
    row = lax.broadcasted_iota(jnp.int32, shape, 0)
    col = lax.broadcasted_iota(jnp.int32, shape, 1)
    frame = (col // 8) * 4 + col % 4 - table[FIRST]
    start = jnp.zeros(shape, jnp.int32)
    end = jnp.zeros(shape, jnp.int32)
    for f in range(4):
        start = jnp.where(row % 4 == f, table[STARTS + f], start)
        end = jnp.where(row % 4 == f, table[ENDS + f], end)
    inside = jnp.logical_and(frame >= start, frame < end)
    mask = jnp.where(jnp.logical_and(inside, row // 4 == (col // 4) % 2), 1.0, 0.0)
    tot = jnp.dot(mask, sums[...], precision=lax.Precision.HIGHEST, preferred_element_type=F32)
    for d in range(o_ref.shape[0]):
        o_ref[d] = tot


def clip_sums(table, sums, down, up, copies):
    return pl.pallas_call(
        clip_kernel,
        in_specs=[SM, VM, ANY, ANY],
        out_specs=[VM, ANY, ANY],
        out_shape=[
            jax.ShapeDtypeStruct((copies, 8, sums.shape[1]), F32),
            jax.ShapeDtypeStruct(down.shape, BF16),
            jax.ShapeDtypeStruct(up.shape, BF16),
        ],
        input_output_aliases={2: 1, 3: 2},
        compiler_params=pltpu.CompilerParams(vmem_limit_bytes=4 * MIB),
        cost_estimate=pl.CostEstimate(flops=LOW, bytes_accessed=LOW, transcendentals=0),
        name="clip_sums",
    )(table, sums, down, up)


def sides_kernel(near, top, bot, mid, sides, sem):
    del near
    copies = [
        pltpu.make_async_copy(src.at[2 + p], sides.at[2 * k + p], sem.at[2 * k + p])
        for k, src in enumerate((top, bot))
        for p in range(2)
    ]
    copies.append(pltpu.make_async_copy(mid, sides.at[pl.ds(4, mid.shape[0])], sem.at[4]))
    for c in copies:
        c.start()
    for c in copies:
        c.wait()


def pack_sides(near, top, bot, mid):
    return pl.pallas_call(
        sides_kernel,
        in_specs=[ANY] * 3 + [HBM],
        out_specs=ANY,
        out_shape=jax.ShapeDtypeStruct((4 + mid.shape[0],) + mid.shape[1:], BF16),
        scratch_shapes=[pltpu.SemaphoreType.DMA((5,))],
        compiler_params=pltpu.CompilerParams(vmem_limit_bytes=4 * MIB),
        cost_estimate=pl.CostEstimate(flops=LOW, bytes_accessed=LOW, transcendentals=0),
        name="pack_sides",
    )(near, top, bot, mid)


def normed_rows(x, half_scale, half_shift):
    u = x.astype(F32) * half_scale + half_shift
    return u + u * jnp.tanh(u)


def put_rows(slab, row, h):
    width, chans = h.shape
    col = lax.broadcasted_iota(jnp.int32, h.shape, 0)
    left = jnp.where(col == 0, 0.0, pltpu.roll(h, 1, 0))
    right = jnp.where(col == width - 1, 0.0, pltpu.roll(h, width - 1, 0))
    slab[row, :, 0:chans] = left.astype(BF16)
    slab[row, :, chans : 2 * chans] = h.astype(BF16)
    slab[row, :, 2 * chans :] = right.astype(BF16)


PAIRS = 8
UPPER, LOWER = range(0, 4), range(4, 8)
TAP0, TAP1, TAP2, TAP01, TAP012, NONE = 0, 1, 2, 3, 4, 5


def bank_kernel(
    clip_len_hbm, owner_hbm, w, sides, page_in, bank, codes, page, clip_len, owner, sems
):
    del sides, page_in, page
    ints = [
        pltpu.make_async_copy(clip_len_hbm, clip_len, sems.at[0]),
        pltpu.make_async_copy(owner_hbm, owner, sems.at[1]),
    ]
    for c in ints:
        c.start()

    def step(i, _):
        r = pl.ds(pl.multiple_of(i * 16, 16), 16)
        taps = [[w[a, b, r].astype(F32) for b in range(3)] for a in range(3)]
        first = [x + y for x, y in zip(taps[0], taps[1])]
        taps += [first, [x + y for x, y in zip(first, taps[2])]]
        for n, (top, mid, low) in enumerate(taps):
            half = 0.5 * (top + low)
            mid = 0.5 * mid
            bank[4 * n, r] = top.astype(BF16)
            bank[4 * n + 1, r] = (half + mid).astype(BF16)
            bank[4 * n + 2, r] = (half - mid).astype(BF16)
            bank[4 * n + 3, r] = low.astype(BF16)
        bank[4 * NONE, r] = jnp.zeros(taps[0][0].shape, BF16)
        return 0

    lax.fori_loop(0, w.shape[2] // 16, step, 0)
    for c in ints:
        c.wait()
    start = jnp.int32(0)
    for i in range(CLIPS):
        for k in range(SEQ_CAP):
            codes[start + k] = owner[i] * SEQ_CAP + k
        start = start + clip_len[i]


def weight_bank(clip_len, owner, weight, sides, page):
    return pl.pallas_call(
        bank_kernel,
        in_specs=[HBM, HBM, VM, ANY, HBM],
        out_specs=[VM, SM, HBM],
        out_shape=[
            jax.ShapeDtypeStruct((4 * NONE + 1,) + weight.shape[2:], BF16),
            jax.ShapeDtypeStruct((64 + SEQ_CAP,), jnp.int32),
            jax.ShapeDtypeStruct(page.shape, BF16),
        ],
        input_output_aliases={4: 2},
        scratch_shapes=[
            pltpu.SMEM((CLIPS,), jnp.int32),
            pltpu.SMEM((CLIPS,), jnp.int32),
            pltpu.SemaphoreType.DMA((2,)),
        ],
        compiler_params=pltpu.CompilerParams(vmem_limit_bytes=16 * MIB),
        cost_estimate=pl.CostEstimate(flops=LOW, bytes_accessed=LOW, transcendentals=0),
        name="weight_bank",
    )(
        pltpu.with_memory_space_constraint(clip_len, pltpu.HBM),
        pltpu.with_memory_space_constraint(owner, pltpu.HBM),
        weight, sides, page,
    )


def lift_steps(row, pairs, hs, hb, top_on, bot_on, page, lifted):
    ring = page.shape[0]
    first, last = 2 * pairs[0], 2 * pairs[-1] + 3

    def normed(r):
        h = normed_rows(row(r - 1), hs, hb)
        if r == 0:
            return h * top_on
        return h * bot_on if r == 2 * PAIRS + 1 else h

    def step(rows):
        for r in rows:
            put_rows(page, r % ring, normed(r))
            if r % 2 == 0 or r == first + 1:
                continue
            p = (r - 3) // 2
            d0, d1, d2, d3 = (page[(2 * p + k) % ring] for k in range(4))
            lifted[0, p] = d0 - d2
            lifted[1, p] = d1 + d2
            lifted[2, p] = d2 - d1
            lifted[3, p] = d3 - d1

    cuts = [first + (last + 1 - first) * i // 4 for i in range(5)]
    return [functools.partial(step, range(cuts[i], cuts[i + 1])) for i in range(4)]


def rows_of(raw, top, bot):
    return lambda r: top[...] if r < 0 else bot[...] if r == 2 * PAIRS else raw(r)


def product(bank, taps, k, pairs, total=None):
    for lifted, pick in taps:
        lhs = lifted[k, pairs[0] : pairs[-1] + 1]
        lhs = lhs.reshape(len(pairs) * lhs.shape[1], lhs.shape[2])
        rhs = bank[jnp.where(pick == NONE, 4 * NONE, 4 * pick + k)]
        d = jnp.dot(lhs, rhs, preferred_element_type=F32)
        total = d if total is None else total + d
    return total


def conv_frame(bank, taps, out, base, beside, pairs=range(PAIRS)):
    r = pl.ds(pairs[0], len(pairs))
    shape = (len(pairs),) + out.shape[2:]
    steps = list(beside) + [lambda: None] * 4
    m1 = product(bank, taps, 1, pairs)
    steps[0]()
    m2 = product(bank, taps, 2, pairs)
    steps[1]()
    even, odd = m1 + m2, m1 - m2
    if base is not None:
        even = even + base[0, r].reshape(even.shape)
        odd = odd + base[1, r].reshape(odd.shape)
    out[0, r] = product(bank, taps, 0, pairs, even).reshape(shape)
    steps[2]()
    out[1, r] = product(bank, taps, 3, pairs, odd).reshape(shape)
    steps[3]()


def pick_taps(start, t):
    return [
        jnp.where(start == t, TAP012, TAP2),
        jnp.where(start <= t - 2, TAP1, jnp.where(start == t - 1, TAP01, NONE)),
        jnp.where(start <= t - 2, TAP0, NONE),
    ]


def finish_steps(conv, feat, cbias_ref, obuf, pairs=range(PAIRS)):
    def step(some):
        for p in some:
            for q in range(2):
                r = 2 * p + q
                total = conv[q, p] + feat[r].astype(F32) + cbias_ref[...]
                obuf[r] = total.astype(BF16)

    n = len(pairs) // 4
    return [functools.partial(step, pairs[n * i : n * i + n]) for i in range(4)]


def spread_latent(proj_ref, pbias_ref, projt, pbias):
    latent_ch, wide = proj_ref.shape[0], projt.shape[1]
    z = lax.broadcasted_iota(jnp.int32, (latent_ch, wide), 0)
    lane = lax.broadcasted_iota(jnp.int32, (latent_ch, wide), 1)
    spread = (lane % latent_ch == z).astype(F32)
    projt[...] = lax.dot_general(
        proj_ref[...], spread.astype(BF16), (((0,), (0,)), ((), ())), preferred_element_type=F32
    ).astype(BF16)
    pbias[...] = jnp.dot(
        pbias_ref[...], spread, precision=lax.Precision.HIGHEST, preferred_element_type=F32
    )


def latent_frame(block, projt, pbias, lscr, lat_ref, f):
    rows, width, chans = block.shape
    wide = projt.shape[1]
    per = wide // 16
    both = jnp.dot(
        block.reshape(rows * width, chans), projt[...], preferred_element_type=F32
    ).reshape(rows, width, wide)
    col = lax.broadcasted_iota(jnp.int32, both.shape, 1)
    lane = lax.broadcasted_iota(jnp.int32, both.shape, 2)
    lscr[...] = jnp.where(col % per == lane // 16, both, 0.0)
    for j in range(width // per):
        part = jnp.sum(lscr[:, per * j : per * (j + 1), :], axis=1) + pbias[...]
        lat_ref[j, f] = part.astype(BF16)


def local_kernel(
    table, feat, top, bot, bank, near, gamma_ref, beta_ref, cbias_ref, proj_ref, pbias_ref,
    block_hbm, part, lat_ref, affine_ref, projt, pbias,
    page, lift0, lift1, lift2, lift3, conv2, conv3, obuf, lscr, osems,
):
    tot = jnp.sum(near[...], axis=0)
    chans = tot.shape[1]
    per = chans // GROUPS
    group = (
        lax.broadcasted_iota(jnp.int32, (chans, chans), 0) // per
        == lax.broadcasted_iota(jnp.int32, (chans, chans), 1) // per
    ).astype(F32)
    tot = jnp.dot(tot, group, precision=lax.Precision.HIGHEST, preferred_element_type=F32)
    for f in range(4):
        count = ((table[ENDS + f] - table[STARTS + f]) * (NH * feat.shape[2] * per)).astype(F32)
        mean = tot[f : f + 1] / count
        var = tot[4 + f : 5 + f] / count - mean * mean
        scale = lax.rsqrt(var + 1e-06) * gamma_ref[...]
        affine_ref[f : f + 1] = 0.5 * scale
        affine_ref[4 + f : 5 + f] = 0.5 * (beta_ref[...] - mean * scale)
    spread_latent(proj_ref, pbias_ref, projt, pbias)

    starts = [table[STARTS + f] for f in range(4)]
    top_on = table[EDGES].astype(F32)
    bot_on = table[EDGES + 1].astype(F32)
    lifts = (lift0, lift1, lift2, lift3)
    picks = [pick_taps(starts[t], t) for t in range(4)]

    def lift(f, pairs=range(PAIRS)):
        return lift_steps(
            rows_of(lambda r: feat[f, r], top.at[f], bot.at[f]), pairs,
            affine_ref[f : f + 1], affine_ref[4 + f : 5 + f], top_on, bot_on, page, lifts[f],
        )

    def taps(t):
        return [(lifts[t - k], picks[t][k]) for k in range(min(t, 2) + 1)]

    def finish(f, conv):
        return finish_steps(conv, feat.at[f], cbias_ref, obuf.at[f - 2])

    def send(f):
        return pltpu.make_async_copy(obuf.at[f - 2], block_hbm.at[f], osems.at[f - 2])

    for step in lift(0, UPPER):
        step()
    conv_frame(bank, taps(0), part.at[0], None, lift(0, LOWER), UPPER)
    conv_frame(bank, taps(0), part.at[0], None, lift(1), LOWER)
    conv_frame(bank, taps(1), part.at[1], None, lift(2))
    conv_frame(bank, taps(2), conv2, None, lift(3))
    conv_frame(bank, taps(3), conv3, None, finish(2, conv2))
    send(2).start()
    for step in finish(3, conv3):
        step()
    send(3).start()
    latent_frame(obuf[0], projt, pbias, lscr, lat_ref, 0)
    latent_frame(obuf[1], projt, pbias, lscr, lat_ref, 1)
    send(2).wait()
    send(3).wait()


def local_part(table, feat, top, bot, bank, near, gamma, beta, cbias, proj, pbias):
    shape = feat.shape
    return pl.pallas_call(
        local_kernel,
        in_specs=[SM] + [VM] * 10,
        out_specs=[ANY, VM, VM, VM, VM, VM],
        out_shape=[
            jax.ShapeDtypeStruct(shape, BF16),
            jax.ShapeDtypeStruct((2, 2, PAIRS) + shape[2:], F32),
            jax.ShapeDtypeStruct((16, 2, 16, 128), BF16),
            jax.ShapeDtypeStruct((8, 256), F32),
            jax.ShapeDtypeStruct((256, 128), BF16),
            jax.ShapeDtypeStruct((1, 128), F32),
        ],
        scratch_shapes=[
            pltpu.VMEM((8, 128, 768), BF16),
            pltpu.VMEM((4, PAIRS, 128, 768), BF16),
            pltpu.VMEM((4, PAIRS, 128, 768), BF16),
            pltpu.VMEM((4, PAIRS, 128, 768), BF16),
            pltpu.VMEM((4, PAIRS, 128, 768), BF16),
            pltpu.VMEM((2, PAIRS, 128, 256), F32),
            pltpu.VMEM((2, PAIRS, 128, 256), F32),
            pltpu.VMEM((2, 16, 128, 256), BF16),
            pltpu.VMEM((16, 128, 128), F32),
            pltpu.SemaphoreType.DMA((2,)),
        ],
        compiler_params=pltpu.CompilerParams(vmem_limit_bytes=LOCAL_VMEM * MIB),
        cost_estimate=pl.CostEstimate(flops=LOW, bytes_accessed=LOW, transcendentals=0),
        name="local_conv",
    )(table, feat, top, bot, bank, near, gamma, beta, cbias, proj, pbias)


def past_affine(table, affine_ref, p):
    on = table[STARTS] < -p
    return jnp.where(on, affine_ref[0:1], 0.0), jnp.where(on, affine_ref[4:5], 0.0)


def one_kernel(
    table, past, sides, feat, bank, part, affine_ref, cbias_ref, projt, pbias, block_in,
    block_hbm, half0, lat_ref,
    page, lift1, lift2, conv1, obuf, lscr, sem,
):
    del block_in
    pick0, pick1 = pick_taps(table[STARTS], 0), pick_taps(table[STARTS + 1], 1)
    on = (table[EDGES].astype(F32), table[EDGES + 1].astype(F32))
    hs, hb = past_affine(table, affine_ref, 0)
    one = rows_of(lambda r: past[AHEAD + r], sides.at[1], sides.at[3])
    for step in lift_steps(one, UPPER, hs, hb, *on, page, lift1):
        step()
    rest = lift_steps(one, LOWER, hs, hb, *on, page, lift1)
    hs, hb = past_affine(table, affine_ref, 1)
    low = rows_of(lambda r: two_row(r, None, sides, past), None, sides.at[2])
    steps = lift_steps(low, LOWER, hs, hb, *on, page, lift2)
    conv_frame(bank, [(lift1, pick1[2])], conv1, part.at[1], rest, UPPER)
    conv_frame(bank, [(lift1, pick1[2])], conv1, part.at[1], steps, LOWER)
    conv_frame(
        bank, [(lift1, pick0[1])], half0, part.at[0],
        finish_steps(conv1, feat.at[1], cbias_ref, obuf),
    )
    out = pltpu.make_async_copy(obuf, block_hbm.at[1], sem)
    out.start()
    conv_frame(bank, [(lift2, pick0[2])], half0, half0, [], LOWER)
    latent_frame(obuf[...], projt, pbias, lscr, lat_ref, 0)
    out.wait()


def two_row(r, late, sides, past):
    if r < LATE:
        return late[r]
    return sides[4 + r - LATE] if r < 2 * PAIRS - AHEAD else past[r - 2 * PAIRS + AHEAD]


def two_kernel(
    table, late, past, sides, feat, bank, half0, affine_ref, cbias_ref, projt, pbias,
    early_ref, one_ref, block_in,
    block_hbm, lat_ref,
    page, lifted, conv0, obuf, lscr, sem,
):
    del block_in
    pick0 = pick_taps(table[STARTS], 0)
    on = (table[EDGES].astype(F32), table[EDGES + 1].astype(F32))
    hs, hb = past_affine(table, affine_ref, 1)
    rows = rows_of(lambda r: two_row(r, late, sides, past), sides.at[0], None)
    for step in lift_steps(rows, UPPER, hs, hb, *on, page, lifted):
        step()
    conv_frame(
        bank, [(lifted, pick0[2])], conv0, half0,
        finish_steps(half0, feat.at[0], cbias_ref, obuf, LOWER), UPPER,
    )
    for step in finish_steps(conv0, feat.at[0], cbias_ref, obuf, UPPER):
        step()
    out = pltpu.make_async_copy(obuf, block_hbm.at[0], sem)
    out.start()
    latent_frame(obuf[...], projt, pbias, lscr, lat_ref, 0)
    lat_ref[:, 1:2] = one_ref[...]
    lat_ref[:, 2:4] = early_ref[...]
    out.wait()


def past_scratch(shape, lifts):
    return [pltpu.VMEM((8, 128, 768), BF16)] + lifts * [
        pltpu.VMEM((4, PAIRS, 128, 768), BF16)
    ] + [
        pltpu.VMEM((2, PAIRS) + shape[2:], F32),
        pltpu.VMEM(shape[1:], BF16),
        pltpu.VMEM((16, 128, 128), F32),
        pltpu.SemaphoreType.DMA,
    ]


def one_part(table, past, sides, feat, bank, part, affine, cbias, proj, pbias, block):
    shape = feat.shape
    return pl.pallas_call(
        one_kernel,
        in_specs=[SM] + [VM] * 9 + [ANY],
        out_specs=[ANY, VM, VM],
        out_shape=[
            jax.ShapeDtypeStruct(shape, BF16),
            jax.ShapeDtypeStruct(part.shape[1:], F32),
            jax.ShapeDtypeStruct((16, 1, 16, 128), BF16),
        ],
        input_output_aliases={10: 0},
        scratch_shapes=past_scratch(shape, 2),
        compiler_params=pltpu.CompilerParams(vmem_limit_bytes=PAST_VMEM * MIB),
        cost_estimate=pl.CostEstimate(flops=LOW, bytes_accessed=LOW, transcendentals=0),
        name="past_one",
    )(table, past, sides, feat, bank, part, affine, cbias, proj, pbias, block)


def two_part(
    table, late, past, sides, feat, bank, half0, affine, cbias, proj, pbias, early, one, block
):
    shape = feat.shape
    return pl.pallas_call(
        two_kernel,
        in_specs=[SM] + [VM] * 12 + [ANY],
        out_specs=[ANY, VM],
        out_shape=[
            jax.ShapeDtypeStruct(shape, BF16),
            jax.ShapeDtypeStruct((16, 4, 16, 128), BF16),
        ],
        input_output_aliases={13: 0},
        scratch_shapes=past_scratch(shape, 1),
        compiler_params=pltpu.CompilerParams(vmem_limit_bytes=PAST_VMEM * MIB),
        cost_estimate=pl.CostEstimate(flops=LOW, bytes_accessed=LOW, transcendentals=0),
        name="past_two",
    )(table, late, past, sides, feat, bank, half0, affine, cbias, proj, pbias, early, one, block)


def place_kernel(codes, x_ref, o_ref):
    o_ref[...] = jnp.zeros_like(o_ref)

    def put(t, _):
        o_ref[codes[t]] = x_ref[t]
        return 0

    lax.fori_loop(0, x_ref.shape[0], put, 0, unroll=8)


def place(codes, shares):
    return pl.pallas_call(
        place_kernel,
        in_specs=[SM, VM],
        out_specs=VM,
        out_shape=jax.ShapeDtypeStruct((128, 16, 128), BF16),
        compiler_params=pltpu.CompilerParams(vmem_limit_bytes=4 * MIB),
        name="place_frames",
    )(codes, shares)


def merge_kernel(x_ref, o_ref):
    for j in range(x_ref.shape[0]):
        o_ref[:, :, 128 * j : 128 * (j + 1)] = x_ref[j]


def merge(seq):
    return pl.pallas_call(
        merge_kernel,
        in_specs=[VM],
        out_specs=VM,
        out_shape=jax.ShapeDtypeStruct((8, 16, 2048), BF16),
        compiler_params=pltpu.CompilerParams(vmem_limit_bytes=4 * MIB),
        name="merge_columns",
    )(seq)


def shift(x, axis, by):
    n = lax.axis_size(axis)
    return lax.ppermute(x, axis, [(i, i + by) for i in range(n) if 0 <= i + by < n])


def on_device(feat, gamma, beta, conv_weight, conv_bias, proj, proj_bias, clip_len, owner):
    frames, band = feat.shape[:2]
    n_time = lax.axis_size("tm")

    sums, table, down, up, one, mid, two = channel_stats(clip_len, feat, n_time)
    sums = lax.all_to_all(sums, "tm", split_axis=0, concat_axis=0, tiled=True)
    one = shift(after(sums, one), "tm", 1)
    sums, down, up = clip_sums(
        table, sums.reshape(-1, sums.shape[-1]), down, up, lax.axis_size("rows")
    )
    top, bot = shift(down, "rows", 1), shift(up, "rows", -1)
    near = lax.all_to_all(sums, "rows", split_axis=0, concat_axis=0, tiled=True)
    sides = pack_sides(near, top, bot, mid)
    bank, codes, two = weight_bank(clip_len, owner, conv_weight, sides, two)
    sides = shift(sides, "tm", 1)
    two = shift(two, "tm", 1)

    cbias, pbias = conv_bias[None, :], proj_bias[None, :]
    block, part, early, affine, projt, ptile = local_part(
        table, feat, top, bot, bank, near, gamma[None, :], beta[None, :], cbias, proj.T,
        pbias,
    )
    block, part, lat = one_part(
        table, one, sides, feat, bank, part, affine, cbias, projt, ptile, block
    )
    block, lat = two_part(
        table, two, one, sides, feat, bank, part, affine, cbias, projt, ptile, early, lat, block
    )
    shares = lax.all_to_all(lat, "tm", split_axis=0, concat_axis=0, tiled=True)
    placed = place(codes, shares.reshape(n_time * frames, band, 128))
    seq = lax.all_to_all(
        placed.reshape(n_time, SEQ_CAP, band, 128), "tm", split_axis=0, concat_axis=0, tiled=True
    )
    return block, merge(seq)


def solution(mesh):
    in_specs = (P("tm", "rows", None, None), P(), P(), P(), P(), P(), P(), P(), P())
    out_specs = (P("tm", "rows", None, None), P("tm", "rows", None))
    return jax.shard_map(
        on_device, mesh=mesh, in_specs=in_specs, out_specs=out_specs, check_vma=False
    )
```

```python
import functools

import jax
import jax.numpy as jnp
from jax import lax
from jax.experimental import pallas as pl
from jax.experimental.pallas import tpu as pltpu
from jax.sharding import PartitionSpec as P

GROUPS = 32
SEQ_CAP = 8
CLIPS = 16
NH = 128
LOW = 1000
LOCAL_VMEM = 35
PAST_VMEM = 26
LATE = 7
AHEAD = 3
F32 = jnp.float32
BF16 = jnp.bfloat16
MIB = 2**20
STARTS, ENDS, EDGES, FIRST, TABLE = 0, 4, 8, 10, 16
ANY = pl.BlockSpec(memory_space=pl.ANY)
VM = pl.BlockSpec(memory_space=pltpu.VMEM)
SM = pl.BlockSpec(memory_space=pltpu.SMEM)
HBM = pl.BlockSpec(memory_space=pltpu.HBM)


def stats_kernel(
    clip_len_hbm, feat, o_ref, table, down_ref, up_ref, one_ref, mid_ref, two_ref, x_ref, sums,
    clip_len, sems, osems, isem,
):
    frames, band = x_ref.shape[:2]
    quarter = band // 4
    split = band - AHEAD
    ints = pltpu.make_async_copy(clip_len_hbm, clip_len, isem)
    ints.start()
    order = [(f, q) for f in (2, 3, 0, 1) for q in range(4)]
    loads = [
        pltpu.make_async_copy(
            feat.at[f, pl.ds(q * quarter, quarter)],
            x_ref.at[f, pl.ds(q * quarter, quarter)],
            sems.at[i],
        )
        for i, (f, q) in enumerate(order)
    ]
    for c in loads:
        c.start()
    onward = {
        2: (
            (x_ref.at[2, pl.ds(split, AHEAD)], one_ref.at[pl.ds(0, AHEAD)]),
            (x_ref.at[2, pl.ds(LATE, split - LATE)], mid_ref),
            (x_ref.at[2, pl.ds(0, LATE)], two_ref),
        ),
        3: ((x_ref.at[3], one_ref.at[pl.ds(AHEAD, band)]),),
        0: (),
        1: (),
    }
    passes = []

    def send_on(src, dst):
        c = pltpu.make_async_copy(src, dst, osems.at[len(passes)])
        c.start()
        passes.append(c)

    first = lax.axis_index("tm") * 4
    row = lax.axis_index("rows")
    table[EDGES] = (row > 0).astype(jnp.int32)
    table[EDGES + 1] = (row < lax.axis_size("rows") - 1).astype(jnp.int32)
    table[FIRST] = first
    starts = [jnp.int32(0)] * 4
    ends = [jnp.int32(0)] * 4
    start = jnp.int32(0)
    for i, (f, q) in enumerate(order):
        if i == CLIPS // 2:
            ints.wait()
        for c in range(max(2 * i - CLIPS, 0), max(2 * i - CLIPS + 2, 0)):
            end = start + clip_len[c]
            for own in range(4):
                inside = jnp.logical_and(first + own >= start, first + own < end)
                starts[own] = jnp.where(inside, start - first, starts[own])
                ends[own] = jnp.where(inside, end - first, ends[own])
            start = end
        loads[i].wait()
        if q == 3:
            down_ref[f] = x_ref[f, band - 1]
            up_ref[f] = x_ref[f, 0]
            for src, dst in onward[f]:
                send_on(src, dst)
        x = x_ref[f, pl.ds(q * quarter, quarter)].astype(F32)
        x = x.reshape(-1, 8, x.shape[-1])
        one = jnp.sum(x, axis=0)
        two = jnp.sum(x * x, axis=0)
        if q == 0:
            sums[f] = one
            sums[4 + f] = two
        else:
            sums[f] += one
            sums[4 + f] += two
    for own in range(4):
        table[STARTS + own] = starts[own]
        table[ENDS + own] = ends[own]
    tot = jnp.sum(sums[...], axis=1)
    for d in range(o_ref.shape[0]):
        o_ref[d] = tot
    for c in passes:
        c.wait()


def channel_stats(clip_len, feat, copies):
    frames, band, width, chans = feat.shape
    return pl.pallas_call(
        stats_kernel,
        in_specs=[HBM, HBM],
        out_specs=[VM, SM, VM, VM, HBM, HBM, HBM],
        out_shape=[
            jax.ShapeDtypeStruct((copies, 2 * frames, chans), F32),
            jax.ShapeDtypeStruct((TABLE,), jnp.int32),
            jax.ShapeDtypeStruct((frames, width, chans), BF16),
            jax.ShapeDtypeStruct((frames, width, chans), BF16),
            jax.ShapeDtypeStruct((band + AHEAD, width, chans), BF16),
            jax.ShapeDtypeStruct((band - AHEAD - LATE, width, chans), BF16),
            jax.ShapeDtypeStruct((LATE, width, chans), BF16),
        ],
        scratch_shapes=[
            pltpu.VMEM(feat.shape, BF16),
            pltpu.VMEM((2 * frames, 8, chans), F32),
            pltpu.SMEM((CLIPS,), jnp.int32),
            pltpu.SemaphoreType.DMA((CLIPS,)),
            pltpu.SemaphoreType.DMA((4,)),
            pltpu.SemaphoreType.DMA,
        ],
        compiler_params=pltpu.CompilerParams(vmem_limit_bytes=16 * MIB),
        cost_estimate=pl.CostEstimate(flops=LOW, bytes_accessed=LOW, transcendentals=0),
        name="channel_stats",
    )(*(pltpu.with_memory_space_constraint(x, pltpu.HBM) for x in (clip_len, feat)))


def after_kernel(sums, page_in, page):
    del sums, page_in, page


def after(sums, page):
    return pl.pallas_call(
        after_kernel,
        in_specs=[ANY, HBM],
        out_specs=HBM,
        out_shape=jax.ShapeDtypeStruct(page.shape, BF16),
        input_output_aliases={1: 0},
        compiler_params=pltpu.CompilerParams(vmem_limit_bytes=4 * MIB),
        cost_estimate=pl.CostEstimate(flops=LOW, bytes_accessed=LOW, transcendentals=0),
        name="after_sums",
    )(sums, page)


def clip_kernel(table, sums, down_in, up_in, o_ref, down, up):
    del down_in, up_in, down, up
    shape = (8, sums.shape[0])
    row = lax.broadcasted_iota(jnp.int32, shape, 0)
    col = lax.broadcasted_iota(jnp.int32, shape, 1)
    frame = (col // 8) * 4 + col % 4 - table[FIRST]
    start = jnp.zeros(shape, jnp.int32)
    end = jnp.zeros(shape, jnp.int32)
    for f in range(4):
        start = jnp.where(row % 4 == f, table[STARTS + f], start)
        end = jnp.where(row % 4 == f, table[ENDS + f], end)
    inside = jnp.logical_and(frame >= start, frame < end)
    mask = jnp.where(jnp.logical_and(inside, row // 4 == (col // 4) % 2), 1.0, 0.0)
    tot = jnp.dot(mask, sums[...], precision=lax.Precision.HIGHEST, preferred_element_type=F32)
    for d in range(o_ref.shape[0]):
        o_ref[d] = tot


def clip_sums(table, sums, down, up, copies):
    return pl.pallas_call(
        clip_kernel,
        in_specs=[SM, VM, ANY, ANY],
        out_specs=[VM, ANY, ANY],
        out_shape=[
            jax.ShapeDtypeStruct((copies, 8, sums.shape[1]), F32),
            jax.ShapeDtypeStruct(down.shape, BF16),
            jax.ShapeDtypeStruct(up.shape, BF16),
        ],
        input_output_aliases={2: 1, 3: 2},
        compiler_params=pltpu.CompilerParams(vmem_limit_bytes=4 * MIB),
        cost_estimate=pl.CostEstimate(flops=LOW, bytes_accessed=LOW, transcendentals=0),
        name="clip_sums",
    )(table, sums, down, up)


def sides_kernel(near, top, bot, mid, sides, sem):
    del near
    copies = [
        pltpu.make_async_copy(src.at[2 + p], sides.at[2 * k + p], sem.at[2 * k + p])
        for k, src in enumerate((top, bot))
        for p in range(2)
    ]
    copies.append(pltpu.make_async_copy(mid, sides.at[pl.ds(4, mid.shape[0])], sem.at[4]))
    for c in copies:
        c.start()
    for c in copies:
        c.wait()


def pack_sides(near, top, bot, mid):
    return pl.pallas_call(
        sides_kernel,
        in_specs=[ANY] * 3 + [HBM],
        out_specs=ANY,
        out_shape=jax.ShapeDtypeStruct((4 + mid.shape[0],) + mid.shape[1:], BF16),
        scratch_shapes=[pltpu.SemaphoreType.DMA((5,))],
        compiler_params=pltpu.CompilerParams(vmem_limit_bytes=4 * MIB),
        cost_estimate=pl.CostEstimate(flops=LOW, bytes_accessed=LOW, transcendentals=0),
        name="pack_sides",
    )(near, top, bot, mid)


def normed_rows(x, half_scale, half_shift):
    u = x.astype(F32) * half_scale + half_shift
    return u + u * jnp.tanh(u)


def put_rows(slab, row, h):
    width, chans = h.shape
    col = lax.broadcasted_iota(jnp.int32, h.shape, 0)
    left = jnp.where(col == 0, 0.0, pltpu.roll(h, 1, 0))
    right = jnp.where(col == width - 1, 0.0, pltpu.roll(h, width - 1, 0))
    slab[row, :, 0:chans] = left.astype(BF16)
    slab[row, :, chans : 2 * chans] = h.astype(BF16)
    slab[row, :, 2 * chans :] = right.astype(BF16)


PAIRS = 8
UPPER, LOWER = range(0, 4), range(4, 8)
TAP0, TAP1, TAP2, TAP01, TAP012, NONE = 0, 1, 2, 3, 4, 5


def bank_kernel(
    clip_len_hbm, owner_hbm, w, sides, page_in, bank, codes, page, clip_len, owner, sems
):
    del sides, page_in, page
    ints = [
        pltpu.make_async_copy(clip_len_hbm, clip_len, sems.at[0]),
        pltpu.make_async_copy(owner_hbm, owner, sems.at[1]),
    ]
    for c in ints:
        c.start()

    def step(i, _):
        r = pl.ds(pl.multiple_of(i * 16, 16), 16)
        taps = [[w[a, b, r].astype(F32) for b in range(3)] for a in range(3)]
        first = [x + y for x, y in zip(taps[0], taps[1])]
        taps += [first, [x + y for x, y in zip(first, taps[2])]]
        for n, (top, mid, low) in enumerate(taps):
            half = 0.5 * (top + low)
            mid = 0.5 * mid
            bank[4 * n, r] = top.astype(BF16)
            bank[4 * n + 1, r] = (half + mid).astype(BF16)
            bank[4 * n + 2, r] = (half - mid).astype(BF16)
            bank[4 * n + 3, r] = low.astype(BF16)
        bank[4 * NONE, r] = jnp.zeros(taps[0][0].shape, BF16)
        return 0

    lax.fori_loop(0, w.shape[2] // 16, step, 0)
    for c in ints:
        c.wait()
    start = jnp.int32(0)
    for i in range(CLIPS):
        for k in range(SEQ_CAP):
            codes[start + k] = owner[i] * SEQ_CAP + k
        start = start + clip_len[i]


def weight_bank(clip_len, owner, weight, sides, page):
    return pl.pallas_call(
        bank_kernel,
        in_specs=[HBM, HBM, VM, ANY, HBM],
        out_specs=[VM, SM, HBM],
        out_shape=[
            jax.ShapeDtypeStruct((4 * NONE + 1,) + weight.shape[2:], BF16),
            jax.ShapeDtypeStruct((64 + SEQ_CAP,), jnp.int32),
            jax.ShapeDtypeStruct(page.shape, BF16),
        ],
        input_output_aliases={4: 2},
        scratch_shapes=[
            pltpu.SMEM((CLIPS,), jnp.int32),
            pltpu.SMEM((CLIPS,), jnp.int32),
            pltpu.SemaphoreType.DMA((2,)),
        ],
        compiler_params=pltpu.CompilerParams(vmem_limit_bytes=16 * MIB),
        cost_estimate=pl.CostEstimate(flops=LOW, bytes_accessed=LOW, transcendentals=0),
        name="weight_bank",
    )(
        pltpu.with_memory_space_constraint(clip_len, pltpu.HBM),
        pltpu.with_memory_space_constraint(owner, pltpu.HBM),
        weight, sides, page,
    )


def lift_steps(row, pairs, hs, hb, top_on, bot_on, page, lifted):
    ring = page.shape[0]
    first, last = 2 * pairs[0], 2 * pairs[-1] + 3

    def normed(r):
        h = normed_rows(row(r - 1), hs, hb)
        if r == 0:
            return h * top_on
        return h * bot_on if r == 2 * PAIRS + 1 else h

    def step(rows):
        for r in rows:
            put_rows(page, r % ring, normed(r))
            if r % 2 == 0 or r == first + 1:
                continue
            p = (r - 3) // 2
            d0, d1, d2, d3 = (page[(2 * p + k) % ring] for k in range(4))
            lifted[0, p] = d0 - d2
            lifted[1, p] = d1 + d2
            lifted[2, p] = d2 - d1
            lifted[3, p] = d3 - d1

    cuts = [first + (last + 1 - first) * i // 4 for i in range(5)]
    return [functools.partial(step, range(cuts[i], cuts[i + 1])) for i in range(4)]


def rows_of(raw, top, bot):
    return lambda r: top[...] if r < 0 else bot[...] if r == 2 * PAIRS else raw(r)


def product(bank, taps, k, pairs, total=None):
    for lifted, pick in taps:
        lhs = lifted[k, pairs[0] : pairs[-1] + 1]
        lhs = lhs.reshape(len(pairs) * lhs.shape[1], lhs.shape[2])
        rhs = bank[jnp.where(pick == NONE, 4 * NONE, 4 * pick + k)]
        d = jnp.dot(lhs, rhs, preferred_element_type=F32)
        total = d if total is None else total + d
    return total


def conv_frame(bank, taps, out, base, beside, pairs=range(PAIRS)):
    r = pl.ds(pairs[0], len(pairs))
    shape = (len(pairs),) + out.shape[2:]
    steps = list(beside) + [lambda: None] * 4
    m1 = product(bank, taps, 1, pairs)
    steps[0]()
    m2 = product(bank, taps, 2, pairs)
    steps[1]()
    even, odd = m1 + m2, m1 - m2
    if base is not None:
        even = even + base[0, r].reshape(even.shape)
        odd = odd + base[1, r].reshape(odd.shape)
    out[0, r] = product(bank, taps, 0, pairs, even).reshape(shape)
    steps[2]()
    out[1, r] = product(bank, taps, 3, pairs, odd).reshape(shape)
    steps[3]()


def pick_taps(start, t):
    return [
        jnp.where(start == t, TAP012, TAP2),
        jnp.where(start <= t - 2, TAP1, jnp.where(start == t - 1, TAP01, NONE)),
        jnp.where(start <= t - 2, TAP0, NONE),
    ]


def finish_steps(conv, feat, cbias_ref, obuf, pairs=range(PAIRS)):
    def step(some):
        for p in some:
            for q in range(2):
                r = 2 * p + q
                total = conv[q, p] + feat[r].astype(F32) + cbias_ref[...]
                obuf[r] = total.astype(BF16)

    n = len(pairs) // 4
    return [functools.partial(step, pairs[n * i : n * i + n]) for i in range(4)]


def spread_latent(proj_ref, pbias_ref, projt, pbias):
    latent_ch, wide = proj_ref.shape[0], projt.shape[1]
    z = lax.broadcasted_iota(jnp.int32, (latent_ch, wide), 0)
    lane = lax.broadcasted_iota(jnp.int32, (latent_ch, wide), 1)
    spread = (lane % latent_ch == z).astype(F32)
    projt[...] = lax.dot_general(
        proj_ref[...], spread.astype(BF16), (((0,), (0,)), ((), ())), preferred_element_type=F32
    ).astype(BF16)
    pbias[...] = jnp.dot(
        pbias_ref[...], spread, precision=lax.Precision.HIGHEST, preferred_element_type=F32
    )


def latent_frame(block, projt, pbias, lscr, lat_ref, f):
    rows, width, chans = block.shape
    wide = projt.shape[1]
    per = wide // 16
    both = jnp.dot(
        block.reshape(rows * width, chans), projt[...], preferred_element_type=F32
    ).reshape(rows, width, wide)
    col = lax.broadcasted_iota(jnp.int32, both.shape, 1)
    lane = lax.broadcasted_iota(jnp.int32, both.shape, 2)
    lscr[...] = jnp.where(col % per == lane // 16, both, 0.0)
    for j in range(width // per):
        part = jnp.sum(lscr[:, per * j : per * (j + 1), :], axis=1) + pbias[...]
        lat_ref[j, f] = part.astype(BF16)


def local_kernel(
    table, feat, top, bot, bank, near, gamma_ref, beta_ref, cbias_ref, proj_ref, pbias_ref,
    block_hbm, part, lat_ref, affine_ref, projt, pbias,
    page, lift0, lift1, lift2, lift3, conv2, conv3, obuf, lscr, osems,
):
    tot = jnp.sum(near[...], axis=0)
    chans = tot.shape[1]
    per = chans // GROUPS
    group = (
        lax.broadcasted_iota(jnp.int32, (chans, chans), 0) // per
        == lax.broadcasted_iota(jnp.int32, (chans, chans), 1) // per
    ).astype(F32)
    tot = jnp.dot(tot, group, precision=lax.Precision.HIGHEST, preferred_element_type=F32)
    for f in range(4):
        count = ((table[ENDS + f] - table[STARTS + f]) * (NH * feat.shape[2] * per)).astype(F32)
        mean = tot[f : f + 1] / count
        var = tot[4 + f : 5 + f] / count - mean * mean
        scale = lax.rsqrt(var + 1e-06) * gamma_ref[...]
        affine_ref[f : f + 1] = 0.5 * scale
        affine_ref[4 + f : 5 + f] = 0.5 * (beta_ref[...] - mean * scale)
    spread_latent(proj_ref, pbias_ref, projt, pbias)

    starts = [table[STARTS + f] for f in range(4)]
    top_on = table[EDGES].astype(F32)
    bot_on = table[EDGES + 1].astype(F32)
    lifts = (lift0, lift1, lift2, lift3)
    picks = [pick_taps(starts[t], t) for t in range(4)]

    def lift(f, pairs=range(PAIRS)):
        return lift_steps(
            rows_of(lambda r: feat[f, r], top.at[f], bot.at[f]), pairs,
            affine_ref[f : f + 1], affine_ref[4 + f : 5 + f], top_on, bot_on, page, lifts[f],
        )

    def taps(t):
        return [(lifts[t - k], picks[t][k]) for k in range(min(t, 2) + 1)]

    def finish(f, conv):
        return finish_steps(conv, feat.at[f], cbias_ref, obuf.at[f - 2])

    def send(f):
        return pltpu.make_async_copy(obuf.at[f - 2], block_hbm.at[f], osems.at[f - 2])

    for step in lift(0, UPPER):
        step()
    conv_frame(bank, taps(0), part.at[0], None, lift(0, LOWER), UPPER)
    conv_frame(bank, taps(0), part.at[0], None, lift(1), LOWER)
    conv_frame(bank, taps(1), part.at[1], None, lift(2))
    conv_frame(bank, taps(2), conv2, None, lift(3))
    conv_frame(bank, taps(3), conv3, None, finish(2, conv2))
    send(2).start()
    for step in finish(3, conv3):
        step()
    send(3).start()
    latent_frame(obuf[0], projt, pbias, lscr, lat_ref, 0)
    latent_frame(obuf[1], projt, pbias, lscr, lat_ref, 1)
    send(2).wait()
    send(3).wait()


def local_part(table, feat, top, bot, bank, near, gamma, beta, cbias, proj, pbias):
    shape = feat.shape
    return pl.pallas_call(
        local_kernel,
        in_specs=[SM] + [VM] * 10,
        out_specs=[ANY, VM, VM, VM, VM, VM],
        out_shape=[
            jax.ShapeDtypeStruct(shape, BF16),
            jax.ShapeDtypeStruct((2, 2, PAIRS) + shape[2:], F32),
            jax.ShapeDtypeStruct((16, 2, 16, 128), BF16),
            jax.ShapeDtypeStruct((8, 256), F32),
            jax.ShapeDtypeStruct((256, 128), BF16),
            jax.ShapeDtypeStruct((1, 128), F32),
        ],
        scratch_shapes=[
            pltpu.VMEM((8, 128, 768), BF16),
            pltpu.VMEM((4, PAIRS, 128, 768), BF16),
            pltpu.VMEM((4, PAIRS, 128, 768), BF16),
            pltpu.VMEM((4, PAIRS, 128, 768), BF16),
            pltpu.VMEM((4, PAIRS, 128, 768), BF16),
            pltpu.VMEM((2, PAIRS, 128, 256), F32),
            pltpu.VMEM((2, PAIRS, 128, 256), F32),
            pltpu.VMEM((2, 16, 128, 256), BF16),
            pltpu.VMEM((16, 128, 128), F32),
            pltpu.SemaphoreType.DMA((2,)),
        ],
        compiler_params=pltpu.CompilerParams(vmem_limit_bytes=LOCAL_VMEM * MIB),
        cost_estimate=pl.CostEstimate(flops=LOW, bytes_accessed=LOW, transcendentals=0),
        name="local_conv",
    )(table, feat, top, bot, bank, near, gamma, beta, cbias, proj, pbias)


def past_affine(table, affine_ref, p):
    on = table[STARTS] < -p
    return jnp.where(on, affine_ref[0:1], 0.0), jnp.where(on, affine_ref[4:5], 0.0)


def one_kernel(
    table, past, sides, feat, bank, part, affine_ref, cbias_ref, projt, pbias, block_in,
    block_hbm, half0, lat_ref,
    page, lift1, lift2, conv1, obuf, lscr, sem,
):
    del block_in
    pick0, pick1 = pick_taps(table[STARTS], 0), pick_taps(table[STARTS + 1], 1)
    on = (table[EDGES].astype(F32), table[EDGES + 1].astype(F32))
    hs, hb = past_affine(table, affine_ref, 0)
    one = rows_of(lambda r: past[AHEAD + r], sides.at[1], sides.at[3])
    for step in lift_steps(one, UPPER, hs, hb, *on, page, lift1):
        step()
    rest = lift_steps(one, LOWER, hs, hb, *on, page, lift1)
    hs, hb = past_affine(table, affine_ref, 1)
    low = rows_of(lambda r: two_row(r, None, sides, past), None, sides.at[2])
    steps = lift_steps(low, LOWER, hs, hb, *on, page, lift2)
    conv_frame(bank, [(lift1, pick1[2])], conv1, part.at[1], rest, UPPER)
    conv_frame(bank, [(lift1, pick1[2])], conv1, part.at[1], steps, LOWER)
    conv_frame(
        bank, [(lift1, pick0[1])], half0, part.at[0],
        finish_steps(conv1, feat.at[1], cbias_ref, obuf),
    )
    out = pltpu.make_async_copy(obuf, block_hbm.at[1], sem)
    out.start()
    conv_frame(bank, [(lift2, pick0[2])], half0, half0, [], LOWER)
    latent_frame(obuf[...], projt, pbias, lscr, lat_ref, 0)
    out.wait()


def two_row(r, late, sides, past):
    if r < LATE:
        return late[r]
    return sides[4 + r - LATE] if r < 2 * PAIRS - AHEAD else past[r - 2 * PAIRS + AHEAD]


def two_kernel(
    table, late, past, sides, feat, bank, half0, affine_ref, cbias_ref, projt, pbias,
    early_ref, one_ref, block_in,
    block_hbm, lat_ref,
    page, lifted, conv0, obuf, lscr, sem,
):
    del block_in
    pick0 = pick_taps(table[STARTS], 0)
    on = (table[EDGES].astype(F32), table[EDGES + 1].astype(F32))
    hs, hb = past_affine(table, affine_ref, 1)
    rows = rows_of(lambda r: two_row(r, late, sides, past), sides.at[0], None)
    for step in lift_steps(rows, UPPER, hs, hb, *on, page, lifted):
        step()
    conv_frame(
        bank, [(lifted, pick0[2])], conv0, half0,
        finish_steps(half0, feat.at[0], cbias_ref, obuf, LOWER), UPPER,
    )
    for step in finish_steps(conv0, feat.at[0], cbias_ref, obuf, UPPER):
        step()
    out = pltpu.make_async_copy(obuf, block_hbm.at[0], sem)
    out.start()
    latent_frame(obuf[...], projt, pbias, lscr, lat_ref, 0)
    lat_ref[:, 1:2] = one_ref[...]
    lat_ref[:, 2:4] = early_ref[...]
    out.wait()


def past_scratch(shape, lifts):
    return [pltpu.VMEM((8, 128, 768), BF16)] + lifts * [
        pltpu.VMEM((4, PAIRS, 128, 768), BF16)
    ] + [
        pltpu.VMEM((2, PAIRS) + shape[2:], F32),
        pltpu.VMEM(shape[1:], BF16),
        pltpu.VMEM((16, 128, 128), F32),
        pltpu.SemaphoreType.DMA,
    ]


def one_part(table, past, sides, feat, bank, part, affine, cbias, proj, pbias, block):
    shape = feat.shape
    return pl.pallas_call(
        one_kernel,
        in_specs=[SM] + [VM] * 9 + [ANY],
        out_specs=[ANY, VM, VM],
        out_shape=[
            jax.ShapeDtypeStruct(shape, BF16),
            jax.ShapeDtypeStruct(part.shape[1:], F32),
            jax.ShapeDtypeStruct((16, 1, 16, 128), BF16),
        ],
        input_output_aliases={10: 0},
        scratch_shapes=past_scratch(shape, 2),
        compiler_params=pltpu.CompilerParams(vmem_limit_bytes=PAST_VMEM * MIB),
        cost_estimate=pl.CostEstimate(flops=LOW, bytes_accessed=LOW, transcendentals=0),
        name="past_one",
    )(table, past, sides, feat, bank, part, affine, cbias, proj, pbias, block)


def two_part(
    table, late, past, sides, feat, bank, half0, affine, cbias, proj, pbias, early, one, block
):
    shape = feat.shape
    return pl.pallas_call(
        two_kernel,
        in_specs=[SM] + [VM] * 12 + [ANY],
        out_specs=[ANY, VM],
        out_shape=[
            jax.ShapeDtypeStruct(shape, BF16),
            jax.ShapeDtypeStruct((16, 4, 16, 128), BF16),
        ],
        input_output_aliases={13: 0},
        scratch_shapes=past_scratch(shape, 1),
        compiler_params=pltpu.CompilerParams(vmem_limit_bytes=PAST_VMEM * MIB),
        cost_estimate=pl.CostEstimate(flops=LOW, bytes_accessed=LOW, transcendentals=0),
        name="past_two",
    )(table, late, past, sides, feat, bank, half0, affine, cbias, proj, pbias, early, one, block)


def place_kernel(codes, x_ref, o_ref):
    o_ref[...] = jnp.zeros_like(o_ref)

    def put(t, _):
        o_ref[codes[t]] = x_ref[t]
        return 0

    lax.fori_loop(0, x_ref.shape[0], put, 0, unroll=8)


def place(codes, shares):
    return pl.pallas_call(
        place_kernel,
        in_specs=[SM, VM],
        out_specs=VM,
        out_shape=jax.ShapeDtypeStruct((128, 16, 128), BF16),
        compiler_params=pltpu.CompilerParams(vmem_limit_bytes=4 * MIB),
        name="place_frames",
    )(codes, shares)


def merge_kernel(x_ref, o_ref, sems):
    copies = [
        pltpu.make_async_copy(x_ref.at[j], o_ref.at[:, :, pl.ds(128 * j, 128)], sems.at[j])
        for j in range(x_ref.shape[0])
    ]
    for c in copies:
        c.start()
    for c in copies:
        c.wait()


def merge(seq):
    return pl.pallas_call(
        merge_kernel,
        in_specs=[ANY],
        out_specs=HBM,
        out_shape=jax.ShapeDtypeStruct((8, 16, 2048), BF16),
        scratch_shapes=[pltpu.SemaphoreType.DMA((16,))],
        compiler_params=pltpu.CompilerParams(vmem_limit_bytes=4 * MIB),
        name="merge_columns",
    )(seq)


def shift(x, axis, by):
    n = lax.axis_size(axis)
    return lax.ppermute(x, axis, [(i, i + by) for i in range(n) if 0 <= i + by < n])


def on_device(feat, gamma, beta, conv_weight, conv_bias, proj, proj_bias, clip_len, owner):
    frames, band = feat.shape[:2]
    n_time = lax.axis_size("tm")

    sums, table, down, up, one, mid, two = channel_stats(clip_len, feat, n_time)
    sums = lax.all_to_all(sums, "tm", split_axis=0, concat_axis=0, tiled=True)
    one = shift(after(sums, one), "tm", 1)
    sums, down, up = clip_sums(
        table, sums.reshape(-1, sums.shape[-1]), down, up, lax.axis_size("rows")
    )
    top, bot = shift(down, "rows", 1), shift(up, "rows", -1)
    near = lax.all_to_all(sums, "rows", split_axis=0, concat_axis=0, tiled=True)
    sides = pack_sides(near, top, bot, mid)
    bank, codes, two = weight_bank(clip_len, owner, conv_weight, sides, two)
    sides = shift(sides, "tm", 1)
    two = shift(two, "tm", 1)

    cbias, pbias = conv_bias[None, :], proj_bias[None, :]
    block, part, early, affine, projt, ptile = local_part(
        table, feat, top, bot, bank, near, gamma[None, :], beta[None, :], cbias, proj.T,
        pbias,
    )
    block, part, lat = one_part(
        table, one, sides, feat, bank, part, affine, cbias, projt, ptile, block
    )
    block, lat = two_part(
        table, two, one, sides, feat, bank, part, affine, cbias, projt, ptile, early, lat, block
    )
    shares = lax.all_to_all(lat, "tm", split_axis=0, concat_axis=0, tiled=True)
    placed = place(codes, shares.reshape(n_time * frames, band, 128))
    seq = lax.all_to_all(
        placed.reshape(n_time, SEQ_CAP, band, 128), "tm", split_axis=0, concat_axis=0, tiled=True
    )
    return block, merge(seq)


def solution(mesh):
    in_specs = (P("tm", "rows", None, None), P(), P(), P(), P(), P(), P(), P(), P())
    out_specs = (P("tm", "rows", None, None), P("tm", "rows", None))
    return jax.shard_map(
        on_device, mesh=mesh, in_specs=in_specs, out_specs=out_specs, check_vma=False
    )
```
